512 devices in a mesh: patch: 128 (over y, z, core), comp: 4 (over x).
Axes of the slice: x: 4, y: 8, z: 8, core: 2. Of those that a mesh axis runs over, the one named last changes fastest.
Arguments:
- vorticity: bfloat16 [128, 3, 32, 1024], P('patch', None, 'comp'), may hold values from -6 to 6
- pair_source: int32 [128, 3], P('patch'), may hold values from 0 to 127, as said below
- pair_offset: int32 [128, 3], P('patch'), may hold values from 0 to 26
- pair_count: int32 [128], P('patch'), may hold values from 1 to 3, as said below
- neighbours: int32 [128, 6], P('patch'), may hold values from -1 to 127, as said below
Outputs:
- velocity: float32 [128, 3, 32, 1024], P('patch', None, 'comp')
- stretching: float32 [128, 3, 32, 1024], P('patch', None, 'comp')
The draws below stay inside these ranges and needn't reach their ends.
Inputs may be any that keep to these rules, and one draw needn't show every extreme that they name: pair_source[t, j] lies within 1 positions of t; the first pair_count[t] slots of a row name different patches, and slots from pair_count[t] on carry no pair. pair_count[t] is at most the number of patches within 1 positions of t, t included. `neighbours`: -1 marks the domain boundary; any other entry is a patch within 1 positions.
All inputs are finite; a program needn't handle non-finite values.
Results may differ from the reference program's by a relative error of at most 0.0035.
The reference program's roundings to bfloat16 on the way (of `tables`, `along_z` and `along_y`) count: a program that leaves them out, or rounds other values in their place, can miss the bound.
Values may be sent and summed in bfloat16 or wider, within the bound.
A program may use at most 64 MiB of HBM per device.

```python
import jax
import jax.numpy as jnp
from jax import lax

CELL = 32
P_DEV = 1
TERMS = 4
NPATCH = 128
NEAR = 3


def draw_pair_source(key, part):
    key = jax.random.fold_in(key, 11)
    score_key, flip_key = jax.random.split(key, 2)
    steps_near = jnp.arange(-P_DEV, P_DEV + 1, dtype=jnp.int32)
    patches = jnp.arange(NPATCH, dtype=jnp.int32)
    targets = patches[:, None] + steps_near[None, :]
    inside = (targets >= 0) & (targets < NPATCH)
    scores = jax.random.randint(score_key, (NPATCH, NEAR), 0, 1 << 20) * NEAR + jnp.arange(NEAR, dtype=jnp.int32)[None, :]
    flip_up = jax.random.randint(flip_key, (NPATCH, 1), 0, 2) == 1
    last_in_block = (patches % P_DEV == P_DEV - 1)[:, None]
    first_in_block = (patches % P_DEV == 0)[:, None]
    upward = (steps_near[None, :] == 1) & last_in_block & inside & (jnp.logical_not(first_in_block) | flip_up)
    downward = (steps_near[None, :] == -1) & first_in_block & inside & (jnp.logical_not(last_in_block) | jnp.logical_not(flip_up))
    scores = jnp.where(upward, -2, scores)
    scores = jnp.where(downward, -1, scores)
    scores = jnp.where(inside, scores, scores + (1 << 28))
    ordering = jnp.argsort(scores, axis=1, stable=True)
    picked = jnp.take_along_axis(targets, ordering, axis=1)
    return jnp.clip(picked, 0, NPATCH - 1).astype(jnp.int32)


def draw_pair_count(key, part):
    key = jax.random.fold_in(key, 23)
    first_key, second_key, third_key = jax.random.split(key, 3)
    patches = jnp.arange(NPATCH, dtype=jnp.int32)
    blocks = patches // P_DEV
    phase = jax.random.randint(first_key, (), 0, 4)
    crowded = (blocks + phase) % 4 == 0
    heavy = NEAR - jax.random.randint(second_key, (NPATCH,), 0, 3)
    lighter = jax.random.randint(third_key, (NPATCH,), 1, NEAR // 3 + 2)
    counts = jnp.where(crowded, heavy, lighter)
    counts = jnp.where(crowded & (patches % P_DEV == 0), NEAR, counts)
    counts = jnp.maximum(counts, 2)
    reachable = jnp.minimum(patches, P_DEV) + jnp.minimum(NPATCH - 1 - patches, P_DEV) + 1
    return jnp.clip(jnp.minimum(counts, reachable), 1, NEAR).astype(jnp.int32)


def draw_neighbours(key, part):
    key = jax.random.fold_in(key, 37)
    first_key, second_key, third_key = jax.random.split(key, 3)
    patches = jnp.arange(NPATCH, dtype=jnp.int32)
    distance = jax.random.randint(first_key, (NPATCH, 6), 1, P_DEV + 1)
    signs = 2 * jax.random.randint(second_key, (NPATCH, 6), 0, 2) - 1
    boundary = jax.random.randint(third_key, (NPATCH, 6), 0, 8) == 0
    others = patches[:, None] + signs * distance
    others = jnp.where(boundary | (others < 0) | (others >= NPATCH), -1, others)
    others = others.at[NPATCH - 1 - P_DEV, 1].set(NPATCH - 1)
    return others.at[0, 0].set(-1).astype(jnp.int32)


def set_ends(values, rng, low, high):
    longest = values.shape.index(max(values.shape))
    spots = []
    for shift in (0, 1):
        where = [jax.random.randint(jax.random.fold_in(rng, axis), (), 0, length) for axis, length in enumerate(values.shape)]
        where[longest] = (where[longest] + shift) % values.shape[longest]
        spots.append(tuple(where))
    return values.at[spots[0]].set(low).at[spots[1]].set(high)


def steps_of(rng, dims, cuts, low, largest):
    gain = 1.0
    for axis_at, blocks in cuts:
        heights = jax.random.uniform(jax.random.fold_in(jax.random.fold_in(rng, 6), axis_at), (blocks,), jnp.float32, low / len(cuts), largest / len(cuts))
        gain = gain * jnp.repeat(jnp.exp(heights), dims[axis_at] // blocks).reshape((-1,) + (1,) * (len(dims) - 1 - axis_at))
    return gain


def centred(rng, extent, width, limit, cuts=(), kind=jnp.bfloat16):
    values = width * jax.random.normal(rng, extent, jnp.float32)
    if cuts:
        values = values * steps_of(rng, extent, cuts, -0.22, 0.18)
    return jnp.clip(values, -limit, limit).astype(kind)


def setup_inputs(seed: int = 0) -> dict:
    key_of = jax.random.split(jax.random.key(seed), 6)
    vorticity = centred(key_of[0], (NPATCH, 3, CELL, CELL * CELL), 1.0, 6.0, ((0, 128), (2, 4)))
    pair_source = draw_pair_source(jax.random.fold_in(key_of[5], 71), 0)
    pair_offset = set_ends(jax.random.randint(key_of[2], (NPATCH, NEAR), 0, 27), jax.random.fold_in(key_of[2], 1), 0, 26).astype(jnp.int32)
    pair_count = draw_pair_count(jax.random.fold_in(key_of[5], 71), 0)
    neighbours = draw_neighbours(jax.random.fold_in(key_of[5], 71), 0)
    return {"vorticity": vorticity, "pair_source": pair_source, "pair_offset": pair_offset, "pair_count": pair_count, "neighbours": neighbours}


OPPOSITE = (1, 0, 3, 2, 5, 4)

def term_weights():
    term_index = jnp.arange(TERMS, dtype=jnp.float32)
    widths = 1.5 * CELL / 4.0 ** (TERMS - 1 - term_index)
    return (widths, 0.08 / jnp.sqrt(widths))

def offset_tables(offset_code):
    widths, weights = term_weights()
    shifts = jnp.stack([offset_code // 9, offset_code // 3 % 3, offset_code % 3]) - 1
    cell_index = jnp.arange(CELL, dtype=jnp.int32)
    spacing = cell_index[None, :, None] - cell_index[None, None, :] - CELL * shifts[:, None, None]
    spacing = spacing.astype(jnp.float32)
    tables = jnp.exp(-spacing[None] ** 2 / (2.0 * widths[:, None, None, None] ** 2))
    return (tables.astype(jnp.bfloat16), weights)

def to_wide(values):
    return lax.optimization_barrier(values.astype(jnp.bfloat16)).astype(jnp.float32)

def pair_field(source, offset_code):
    tables, weights = offset_tables(offset_code)
    tables = tables.astype(jnp.float32)
    highest = lax.Precision.HIGHEST
    along_z = to_wide(jnp.einsum('kab,ixyb->kixya', tables[:, 2], source.astype(jnp.float32), precision=highest))
    along_y = to_wide(jnp.einsum('kab,kixbz->kixaz', tables[:, 1], along_z, precision=highest))
    along_x = jnp.einsum('kab,kibyz->kiayz', tables[:, 0], along_y, precision=highest)
    return lax.optimization_barrier(jnp.sum(weights[:, None, None, None, None] * along_x, axis=0))

def faces_of(values):
    return jnp.stack([values[:, 0], values[:, -1], values[:, :, 0], values[:, :, -1], values[:, :, :, 0], values[:, :, :, -1]])

def ghosts_of(window_faces, neighbour_rows, window_start):
    flipped = jnp.array(OPPOSITE, dtype=jnp.int32)
    position = jnp.clip(neighbour_rows - window_start, 0, window_faces.shape[0] - 1)
    picked = window_faces[position, flipped]
    return jnp.where((neighbour_rows >= 0)[:, None, None, None], picked, 0.0)

def difference(values, ghosts, direction):
    lower_side = jnp.expand_dims(ghosts[2 * direction - 2], direction)
    higher = jnp.expand_dims(ghosts[2 * direction - 1], direction)
    padded = jnp.concatenate([lower_side, values, higher], axis=direction)
    length = values.shape[direction]
    return 0.5 * (lax.slice_in_dim(padded, 2, length + 2, axis=direction) - lax.slice_in_dim(padded, 0, length, axis=direction))

def curl_of(values, ghosts):
    grad_x, grad_y, grad_z = [difference(values, ghosts, direction) for direction in (1, 2, 3)]
    return jnp.stack([grad_y[2] - grad_z[1], grad_z[0] - grad_x[2], grad_x[1] - grad_y[0]])

def stretch_of(velocity, ghosts, vortex):
    grad_x, grad_y, grad_z = [difference(velocity, ghosts, direction) for direction in (1, 2, 3)]
    return vortex[0] * grad_x + vortex[1] * grad_y + vortex[2] * grad_z

def reference(vorticity, pair_source, pair_offset, pair_count, neighbours):
    fields = vorticity.reshape(NPATCH, 3, CELL, CELL, CELL)

    def one_target(packed_row):
        sources, offsets, live_count = packed_row

        def add_pair(slot_id, running):
            source = lax.dynamic_index_in_dim(fields, sources[slot_id], 0, keepdims=False)
            return running + pair_field(source, offsets[slot_id])
        return lax.fori_loop(0, live_count, add_pair, jnp.zeros((3, CELL, CELL, CELL), jnp.float32))
    potential = lax.map(one_target, (pair_source, pair_offset, pair_count))
    potential_faces = jax.vmap(faces_of)(potential)
    potential_ghosts = jax.vmap(lambda neighbour_rows: ghosts_of(potential_faces, neighbour_rows, 0))(neighbours)
    velocity = lax.map(lambda paired: curl_of(paired[0], paired[1]), (potential, potential_ghosts))
    velocity_faces = jax.vmap(faces_of)(velocity)
    velocity_ghosts = jax.vmap(lambda neighbour_rows: ghosts_of(velocity_faces, neighbour_rows, 0))(neighbours)
    stretching = lax.map(lambda triple: stretch_of(triple[0], triple[1], triple[2].astype(jnp.float32)), (velocity, velocity_ghosts, fields))
    out_shape = (NPATCH, 3, CELL, CELL * CELL)
    return (velocity.reshape(out_shape), stretching.reshape(out_shape))
```

```python
import functools

import jax
import jax.numpy as jnp
from jax import lax
from jax.experimental import pallas as pl
from jax.experimental.pallas import tpu as pltpu
from jax.sharding import PartitionSpec as P

CELL = 32
TERMS = 4
NEAR = 3
MEMBERS = 4
SLAB = CELL // MEMBERS
COMPONENTS = 3
CHUNK = 4 * COMPONENTS * SLAB
PATCH_ROWS = MEMBERS * CHUNK
TILE = 256
HALO = 16
W0 = 0.08 / 0.75 ** 0.5
F32 = jnp.float32
BF16 = jnp.bfloat16
MESH_ID = pl.DeviceIdType.MESH


def iota(shape, dim):
    return lax.broadcasted_iota(jnp.int32, shape, dim)


def lane_roll(values, shift):
    shift = shift % 128
    return values if shift == 0 else pltpu.roll(values, shift, values.ndim - 1)


def row_roll(values, shift):
    shift = shift % 8
    if shift == 0:
        return values
    grouped = values.reshape(-1, 8, 128)
    return pltpu.roll(grouped, shift, 1).reshape(values.shape)


def slot_of(position, src_ref, off_ref, cnt_ref, patch):
    code = jnp.int32(13)
    live = jnp.int32(0)
    count = cnt_ref[0]
    for j in range(NEAR):
        hit = (count > j) & (src_ref[0, j] == patch - 1 + position)
        code = jnp.where(hit, off_ref[0, j], code)
        live = jnp.where(hit, 1, live)
    shifts = (lax.div(code, 9) - 1, lax.rem(lax.div(code, 3), 3) - 1, lax.rem(code, 3) - 1)
    return shifts, live


def gauss(spacing, scale):
    spacing = spacing.astype(F32)
    return jnp.exp(-(spacing * spacing / 1.125) * scale)


def write_tables(position, shifts, live, member, wz_ref, wy_ref, lx_ref):
    shift_x, shift_y, shift_z = shifts
    rows = iota((CELL, TILE), 0)
    cols = iota((CELL, TILE), 1)
    gap_z = (cols >> 3) - rows - CELL * shift_z
    gap_y = ((cols >> 5) + 8 * ((cols >> 3) & 3)) - rows - CELL * shift_y
    low = cols & 7
    low8 = iota((8, TILE), 1) & 7
    for k in range(TERMS):
        scale = 1.0 / 16.0 ** k
        table = gauss(gap_z, scale)
        wz_ref[position * TERMS + k] = jnp.concatenate(
            [jnp.where(low == y, table, 0.0) for y in range(8)], axis=0
        ).astype(BF16)
        table = gauss(gap_y, scale)
        wy_ref[position * TERMS + k] = jnp.concatenate(
            [jnp.where(low8 == z, table[8 * h : 8 * h + 8], 0.0) for h in range(4) for z in range(8)],
            axis=0,
        ).astype(BF16)
    row = iota((HALO, 128), 0)
    col = iota((HALO, 128), 1)
    plane = (SLAB * member + jnp.where(row < 12, row, row - HALO)) & (CELL - 1)
    term = col >> 5
    scale = jnp.where(term == 0, 1.0, jnp.where(term == 1, 1 / 16, jnp.where(term == 2, 1 / 256, 1 / 4096)))
    weight = jnp.where(term == 0, 1.0, jnp.where(term == 1, 0.5, jnp.where(term == 2, 0.25, 0.125)))
    table = gauss(plane - (col & (CELL - 1)) - CELL * shift_x, scale).astype(BF16).astype(F32)
    lx_ref[position] = (table * weight * live.astype(F32)).astype(BF16)


def pair_products(position, gbuf, wz_ref, wy_ref, lx_ref, rbuf, acc, first):
    lower = iota((MEMBERS, 24, 128), 2) < 64
    for k in range(TERMS):
        along_z = jnp.dot(gbuf[position], wz_ref[position * TERMS + k], preferred_element_type=F32)
        along_z = along_z.reshape(MEMBERS, 4, 24, TILE)
        blocks = [[None] * 2 for _ in range(4)]
        for pair in range(2):
            for half in range(2):
                a = along_z[:, 2 * pair, :, 128 * half : 128 * half + 128]
                b = along_z[:, 2 * pair + 1, :, 128 * half : 128 * half + 128]
                blocks[2 * half][pair] = jnp.where(lower, a, lane_roll(b, 64))
                blocks[2 * half + 1][pair] = jnp.where(lower, lane_roll(a, 64), b)
        pieces = []
        for block in blocks:
            joined = jnp.concatenate(block, axis=2)
            for i in range(COMPONENTS):
                pieces.append(joined[:, 8 * i : 8 * i + 8].reshape(CELL, TILE))
        swapped = jnp.concatenate(pieces, axis=0).astype(BF16)
        along_y = jnp.dot(swapped, wy_ref[position * TERMS + k], preferred_element_type=F32).astype(BF16)
        rbuf[:, CELL * k : CELL * k + CELL, :] = along_y.reshape(12, CELL, TILE)
    for block in range(12):
        term = jnp.dot(lx_ref[position], rbuf[block], preferred_element_type=F32)
        acc[block] = term if first else acc[block] + term


def potential_of(acc):
    lane = iota((2 * HALO, 128), 1)
    bit4 = (lane & 16) == 0
    bit3 = (lane & 8) == 0
    out = []
    for i in range(COMPONENTS):
        a = []
        for block in range(4):
            tile = acc[3 * block + i] * W0
            a.append(jnp.concatenate([tile[:, :128], tile[:, 128:]], axis=0))
        b = [
            jnp.where(bit4, a[0], lane_roll(a[2], 16)),
            jnp.where(bit4, a[1], lane_roll(a[3], 16)),
            jnp.where(bit4, lane_roll(a[0], -16), a[2]),
            jnp.where(bit4, lane_roll(a[1], -16), a[3]),
        ]
        d = [
            jnp.where(bit3, b[0], lane_roll(b[1], 8)),
            jnp.where(bit3, lane_roll(b[0], -8), b[1]),
            jnp.where(bit3, b[2], lane_roll(b[3], 8)),
            jnp.where(bit3, lane_roll(b[2], -8), b[3]),
        ]
        out.append(jnp.concatenate(d, axis=0))
    return out


def z_slots(count):
    for j in range(count):
        for v in range(8):
            yield j, v, v % 2, 2 * (count * (v // 2) + j) + 1


def pack_z(fields, rows):
    shape = (rows, 128)
    lane = iota(shape, 1) & 31
    packed = [jnp.zeros(shape, F32)] * 2
    for j, v, u, s in z_slots(len(fields)):
        mine = (lane == s) | (lane == s - 1)
        packed[u] = jnp.where(mine, lane_roll(fields[j][rows * v : rows * v + rows], s), packed[u])
    return packed


def unpack_z(packed, count, rows):
    above = [[None] * 8 for _ in range(count)]
    below = [[None] * 8 for _ in range(count)]
    for j, v, u, s in z_slots(count):
        above[j][v] = lane_roll(packed[u], 31 - s)
        below[j][v] = lane_roll(packed[u], 97 - s)
    return (
        [jnp.concatenate(x, axis=0) for x in above],
        [jnp.concatenate(x, axis=0) for x in below],
    )


def grad_z(field, above, below):
    z = iota(field.shape, 1) & 31
    higher = jnp.where(z == 31, above, lane_roll(field, -1))
    lower = jnp.where(z == 0, below, lane_roll(field, 1))
    return 0.5 * (higher - lower)


def pack_y(field, rows):
    lower = iota((rows, 128), 1) < 64
    return jnp.where(lower, field[:rows], field[7 * rows :])


def grad_y(field, ghost, rows):
    lane = iota(field.shape, 1)
    moved = lane_roll(field, -32)
    following = jnp.concatenate([moved[rows:], lane_roll(ghost, -32)], axis=0)
    higher = jnp.where(lane < 96, moved, following)
    moved = lane_roll(field, 32)
    previous = jnp.concatenate([lane_roll(ghost, 32), moved[:-rows]], axis=0)
    lower = jnp.where(lane >= 32, moved, previous)
    return 0.5 * (higher - lower)


def halves(field):
    grouped = field.reshape(8, 2, 8, 128)
    return grouped[:, 0], grouped[:, 1]


def pack_x(fields, member):
    groups = []
    for field in fields:
        low, high = halves(field)
        at_end = jnp.full(low.shape, member, jnp.int32) == MEMBERS - 1
        first = jnp.where(at_end, high, low)
        last = jnp.where(at_end, low, high)
        row = iota((2, 8, 128), 1)
        packed = jnp.zeros((2, 8, 128), F32)
        for s in range(4):
            a = pltpu.roll(first[2 * s : 2 * s + 2], 7 - s, 1)
            b = pltpu.roll(last[2 * s : 2 * s + 2], s + 1, 1)
            packed = jnp.where(row == 7 - s, a, jnp.where(row == s, b, packed))
        groups.append(packed)
    return groups


def unpack_x(packed):
    above = jnp.concatenate([packed if s == 0 else pltpu.roll(packed, s, 1) for s in range(4)], axis=0)
    below = jnp.concatenate([packed if s == 0 else pltpu.roll(packed, 8 - s, 1) for s in range(4)], axis=0)
    return above, below


def grad_x(field, packed, member, own_only):
    low, high = halves(field)
    above, below = unpack_x(packed)
    row = iota(low.shape, 1)
    device = jnp.full(low.shape, member, jnp.int32)
    first = device == 0
    last = device == MEMBERS - 1
    moved_low = pltpu.roll(low, 7, 1)
    moved_high = pltpu.roll(high, 7, 1)
    up_low = jnp.where(row == 7, jnp.where(last, above, moved_high), moved_low)
    back_low = pltpu.roll(low, 1, 1)
    back_high = pltpu.roll(high, 1, 1)
    down_low = jnp.where(row == 0, jnp.where(first, below, back_high), back_low)
    own = 0.5 * (up_low - down_low)
    if own_only:
        return own.reshape(64, 128)
    up_high = jnp.where(row == 7, jnp.where(first, above, moved_low), moved_high)
    down_high = jnp.where(row == 0, jnp.where(last, below, back_low), back_high)
    other = 0.5 * (up_high - down_high)
    return jnp.stack([own, other], axis=1).reshape(128, 128)


def own_rows(field):
    return halves(field)[0].reshape(64, 128)


def kernel(patches, src_ref, off_ref, cnt_ref, nb_ref, vort_ref, vel_ref, str_ref,
           gbuf, wz_ref, wy_ref, lx_ref, rbuf, acc, pbuf, vbuf,
           xsend, fsend, grecv, psend, precv, vsend, vrecv):
    patch = lax.axis_index("patch")
    member = lax.axis_index("comp")
    left = lax.rem(patch + patches - 1, patches)
    right = lax.rem(patch + 1, patches)

    def chunk(position, owner):
        return gbuf.at[position, pl.ds(pl.multiple_of(owner * CHUNK, CHUNK), CHUNK)]

    def other(step):
        return lax.rem(member + step, MEMBERS)

    barrier = pltpu.get_barrier_semaphore()
    partners = [(patch, other(d)) for d in (1, 2, 3)] + [(left, member), (right, member)]
    for partner in partners:
        pl.semaphore_signal(barrier, inc=1, device_id=partner, device_id_type=MESH_ID)

    cells = [vort_ref[0, i].astype(F32) for i in range(COMPONENTS)]
    staged = jnp.concatenate(
        [cells[i][:, TILE * q : TILE * q + TILE] for q in range(4) for i in range(COMPONENTS)], axis=0
    ).astype(BF16)
    gbuf[1, pl.ds(pl.multiple_of(member * CHUNK, CHUNK), CHUNK), :] = staged
    pl.semaphore_wait(barrier, len(partners))

    def across(step):
        return pltpu.make_async_remote_copy(
            src_ref=chunk(1, member), dst_ref=chunk(1, member),
            send_sem=xsend.at[step - 1], recv_sem=grecv.at[MEMBERS + member],
            device_id=(patch, other(step)), device_id_type=MESH_ID,
        )

    def onward(owner, step):
        target, place = ((right, 0), (left, 2))[step]
        return pltpu.make_async_remote_copy(
            src_ref=chunk(1, owner), dst_ref=chunk(place, owner),
            send_sem=fsend.at[2 * owner + step], recv_sem=grecv.at[place * MEMBERS + owner],
            device_id=(target, member), device_id_type=MESH_ID,
        )

    def arrived(position, owner):
        pltpu.make_async_remote_copy(
            src_ref=chunk(position, owner), dst_ref=chunk(position, owner),
            send_sem=xsend.at[0], recv_sem=grecv.at[position * MEMBERS + owner],
            device_id=(right, member), device_id_type=MESH_ID,
        ).wait_recv()

    across(1).start()
    across(3).start()
    onward(member, 0).start()
    onward(member, 1).start()
    across(2).start()

    def tables(position):
        shifts, live = slot_of(position, src_ref, off_ref, cnt_ref, patch)
        write_tables(position, shifts, live, member, wz_ref, wy_ref, lx_ref)

    def products(position, first):
        pair_products(position, gbuf, wz_ref, wy_ref, lx_ref, rbuf, acc, first)

    tables(1)
    for step in (1, 3, 2):
        owner = other(step)
        arrived(1, owner)
        onward(owner, 0).start()
        onward(owner, 1).start()
    tables(0)
    tables(2)
    products(1, True)
    for position in (0, 2):
        for step in (0, 1, 3, 2):
            arrived(position, other(step))
        products(position, False)

    def exchange(buffer, send, recv):
        copies = []
        for step, (target, place) in enumerate(((right, 0), (left, 2))):
            copies.append(pltpu.make_async_remote_copy(
                src_ref=buffer.at[1], dst_ref=buffer.at[place],
                send_sem=send.at[step], recv_sem=recv.at[step],
                device_id=(target, member), device_id_type=MESH_ID,
            ))
        for copy in copies:
            copy.start()
        return copies

    def pick(buffer, face, index, shape):
        source = jnp.full(shape, nb_ref[0, face], jnp.int32)
        parts = [buffer[place, index].reshape(shape) for place in range(3)]
        chosen = jnp.where(source < patch, parts[0], jnp.where(source == patch, parts[1], parts[2]))
        return jnp.where(source < 0, 0.0, chosen)

    def ghosts(buffer, rows, z_count, y_count, x_count):
        shape = (rows, 128)
        groups = rows // 8
        lane = iota(shape, 1)
        zs, ys, xs = [], [], []
        for u in range(2):
            index = pl.ds(u * groups, groups)
            zs.append(jnp.where((lane & 1) == 1, pick(buffer, 5, index, shape), pick(buffer, 4, index, shape)))
        at = 2 * groups
        for j in range(y_count):
            index = pl.ds(at, groups)
            ys.append(jnp.where(lane < 64, pick(buffer, 3, index, shape), pick(buffer, 2, index, shape)))
            at += groups
        shape = (2, 8, 128)
        row = iota(shape, 1)
        for j in range(x_count):
            index = pl.ds(at, 2)
            xs.append(jnp.where(row < 4, pick(buffer, 0, index, shape), pick(buffer, 1, index, shape)))
            at += 2
        return zs, ys, xs

    px, py, pz = potential_of(acc)
    packs = pack_z([px, py], HALO) + [pack_y(px, HALO), pack_y(pz, HALO)]
    for index, part in enumerate(packs):
        pbuf[1, 2 * index : 2 * index + 2] = part.reshape(2, 8, 128)
    for index, part in enumerate(pack_x([py, pz], member)):
        pbuf[1, 8 + 2 * index : 10 + 2 * index] = part
    copies = exchange(pbuf, psend, precv)
    for copy in copies:
        copy.wait_recv()
    zs, ys, xs = ghosts(pbuf, HALO, 2, 2, 2)
    above, below = unpack_z(zs, 2, HALO)
    vx = grad_y(pz, ys[1], HALO) - grad_z(py, above[1], below[1])
    vy = grad_z(px, above[0], below[0]) - grad_x(pz, xs[1], member, False)
    vz = grad_x(py, xs[0], member, False) - grad_y(px, ys[0], HALO)
    velocity = [vx, vy, vz]
    own = [own_rows(v) for v in velocity]
    packs = pack_z(own, 8) + [pack_y(v, 8) for v in own]
    for index, part in enumerate(packs):
        vbuf[1, index] = part
    for index, part in enumerate(pack_x(velocity, member)):
        vbuf[1, 5 + 2 * index : 7 + 2 * index] = part
    vcopies = exchange(vbuf, vsend, vrecv)
    for i in range(COMPONENTS):
        for v in range(8):
            vel_ref[0, i, :, 128 * v : 128 * v + 128] = own[i][8 * v : 8 * v + 8]
    for copy in vcopies:
        copy.wait_recv()
    zs, ys, xs = ghosts(vbuf, 8, 3, 3, 3)
    above, below = unpack_z(zs, 3, 8)
    spin = [
        jnp.concatenate([vort_ref[0, i, :, 128 * v : 128 * v + 128].astype(F32) for v in range(8)], axis=0)
        for i in range(COMPONENTS)
    ]
    for i in range(COMPONENTS):
        total = (
            spin[0] * grad_x(velocity[i], xs[i], member, True)
            + spin[1] * grad_y(own[i], ys[i], 8)
            + spin[2] * grad_z(own[i], above[i], below[i])
        )
        for v in range(8):
            str_ref[0, i, :, 128 * v : 128 * v + 128] = total[8 * v : 8 * v + 8]

    for step in (1, 2, 3):
        across(step).wait_send()
    for owner in range(MEMBERS):
        onward(owner, 0).wait_send()
        onward(owner, 1).wait_send()
    for copy in copies + vcopies:
        copy.wait_send()


def body(patches, vorticity, pair_source, pair_offset, pair_count, neighbours):
    smem = pl.BlockSpec(memory_space=pltpu.SMEM)
    vmem = pl.BlockSpec(memory_space=pltpu.VMEM)
    out = jax.ShapeDtypeStruct((1, COMPONENTS, SLAB, CELL * CELL), F32)
    return pl.pallas_call(
        functools.partial(kernel, patches),
        out_shape=(out, out),
        in_specs=[smem, smem, smem, smem, vmem],
        out_specs=(vmem, vmem),
        scratch_shapes=[
            pltpu.VMEM((3, PATCH_ROWS, TILE), BF16),
            pltpu.VMEM((3 * TERMS, TILE, TILE), BF16),
            pltpu.VMEM((3 * TERMS, TILE, TILE), BF16),
            pltpu.VMEM((3, HALO, 128), BF16),
            pltpu.VMEM((12, 128, TILE), BF16),
            pltpu.VMEM((12, HALO, TILE), F32),
            pltpu.VMEM((3, 12, 8, 128), F32),
            pltpu.VMEM((3, 11, 8, 128), F32),
            pltpu.SemaphoreType.DMA((3,)),
            pltpu.SemaphoreType.DMA((2 * MEMBERS,)),
            pltpu.SemaphoreType.DMA((3 * MEMBERS,)),
            pltpu.SemaphoreType.DMA((2,)),
            pltpu.SemaphoreType.DMA((2,)),
            pltpu.SemaphoreType.DMA((2,)),
            pltpu.SemaphoreType.DMA((2,)),
        ],
        compiler_params=pltpu.CompilerParams(
            collective_id=0, has_side_effects=True, vmem_limit_bytes=40 * 1024 * 1024
        ),
    )(pair_source, pair_offset, pair_count, neighbours, vorticity)


def solution(mesh):
    return jax.shard_map(
        functools.partial(body, mesh.shape["patch"]),
        mesh=mesh,
        in_specs=(
            P("patch", None, "comp", None),
            P("patch", None),
            P("patch", None),
            P("patch"),
            P("patch", None),
        ),
        out_specs=(P("patch", None, "comp", None), P("patch", None, "comp", None)),
        check_vma=False,
    )
```

```python
import functools

import jax
import jax.numpy as jnp
from jax import lax
from jax.experimental import pallas as pl
from jax.experimental.pallas import tpu as pltpu
from jax.sharding import PartitionSpec as P

CELL = 32
TERMS = 4
NEAR = 3
MEMBERS = 4
SLAB = CELL // MEMBERS
COMPONENTS = 3
CHUNK = 4 * COMPONENTS * SLAB
PATCH_ROWS = MEMBERS * CHUNK
TILE = 256
HALO = 16
W0 = 0.08 / 0.75 ** 0.5
F32 = jnp.float32
BF16 = jnp.bfloat16
MESH_ID = pl.DeviceIdType.MESH
STEPS = (0, 1, 3, 2)
SLOT = {step: slot for slot, step in enumerate(STEPS)}
PARTS = (1, 1, 2)


def iota(shape, dim):
    return lax.broadcasted_iota(jnp.int32, shape, dim)


def lane_roll(values, shift):
    shift = shift % 128
    return values if shift == 0 else pltpu.roll(values, shift, values.ndim - 1)


def row_roll(values, shift):
    shift = shift % 8
    if shift == 0:
        return values
    grouped = values.reshape(-1, 8, 128)
    return pltpu.roll(grouped, shift, 1).reshape(values.shape)


def slot_of(source, src_ref, off_ref, cnt_ref):
    code = jnp.int32(13)
    live = jnp.int32(0)
    count = cnt_ref[0]
    for j in range(NEAR):
        hit = (count > j) & (src_ref[0, j] == source)
        code = jnp.where(hit, off_ref[0, j], code)
        live = jnp.where(hit, 1, live)
    shifts = (lax.div(code, 9) - 1, lax.rem(lax.div(code, 3), 3) - 1, lax.rem(code, 3) - 1)
    return shifts, live


def gauss(spacing, scale):
    spacing = spacing.astype(F32)
    return jnp.exp(-(spacing * spacing / 1.125) * scale)


def write_tables(position, shifts, live, member, wz_ref, wy_ref, lx_ref):
    shift_x, shift_y, shift_z = shifts
    rows = iota((CELL, TILE), 0)
    cols = iota((CELL, TILE), 1)
    gap_z = (cols >> 3) - rows - CELL * shift_z
    gap_y = ((cols >> 5) + 8 * ((cols >> 3) & 3)) - rows - CELL * shift_y
    low = cols & 7
    low8 = iota((8, TILE), 1) & 7
    for k in range(TERMS):
        scale = 1.0 / 16.0 ** k
        table = gauss(gap_z, scale)
        wz_ref[position * TERMS + k] = jnp.concatenate(
            [jnp.where(low == y, table, 0.0) for y in range(8)], axis=0
        ).astype(BF16)
        table = gauss(gap_y, scale)
        wy_ref[position * TERMS + k] = jnp.concatenate(
            [jnp.where(low8 == z, table[8 * h : 8 * h + 8], 0.0) for h in range(4) for z in range(8)],
            axis=0,
        ).astype(BF16)
    row = iota((HALO, 128), 0)
    col = iota((HALO, 128), 1)
    plane = (SLAB * member + jnp.where(row < 12, row, row - HALO)) & (CELL - 1)
    if PARTS[position] == 1:
        term = col >> 5
        slot = (col >> 3) & 3
    else:
        term = (col >> 4) & 3
        slot = 2 * (col >> 6) + ((col >> 3) & 1)
    step = slot ^ (slot >> 1)
    source = SLAB * ((member + step) & 3) + (col & 7)
    scale = jnp.where(term == 0, 1.0, jnp.where(term == 1, 1 / 16, jnp.where(term == 2, 1 / 256, 1 / 4096)))
    weight = jnp.where(term == 0, 1.0, jnp.where(term == 1, 0.5, jnp.where(term == 2, 0.25, 0.125)))
    table = gauss(plane - source - CELL * shift_x, scale).astype(BF16).astype(F32)
    lx_ref[position] = (table * weight * live.astype(F32)).astype(BF16)


def zy_products(position, part, gbuf, wz_ref, wy_ref, rbuf):
    slots = MEMBERS // PARTS[position]
    rows = slots * CHUNK
    lower = iota((slots, 24, 128), 2) < 64
    for k in range(TERMS):
        along_z = jnp.dot(
            gbuf[position, part * rows : part * rows + rows],
            wz_ref[position * TERMS + k],
            preferred_element_type=F32,
        ).reshape(slots, 4, 24, TILE)
        blocks = [[None] * 2 for _ in range(4)]
        for pair in range(2):
            for half in range(2):
                a = along_z[:, 2 * pair, :, 128 * half : 128 * half + 128]
                b = along_z[:, 2 * pair + 1, :, 128 * half : 128 * half + 128]
                blocks[2 * half][pair] = jnp.where(lower, a, lane_roll(b, 64))
                blocks[2 * half + 1][pair] = jnp.where(lower, lane_roll(a, 64), b)
        pieces = []
        for block in blocks:
            joined = jnp.concatenate(block, axis=2)
            for i in range(COMPONENTS):
                pieces.append(joined[:, 8 * i : 8 * i + 8].reshape(8 * slots, TILE))
        swapped = jnp.concatenate(pieces, axis=0).astype(BF16)
        along_y = jnp.dot(swapped, wy_ref[position * TERMS + k], preferred_element_type=F32).astype(BF16)
        at = (part * TERMS + k) * 8 * slots
        rbuf[:, at : at + 8 * slots, :] = along_y.reshape(12, 8 * slots, TILE)


def x_products(position, lx_ref, rbuf, acc, first):
    for block in range(12):
        term = jnp.dot(lx_ref[position], rbuf[block], preferred_element_type=F32)
        acc[block] = term if first else acc[block] + term


def potential_of(acc):
    lane = iota((2 * HALO, 128), 1)
    bit4 = (lane & 16) == 0
    bit3 = (lane & 8) == 0
    out = []
    for i in range(COMPONENTS):
        a = []
        for block in range(4):
            tile = acc[3 * block + i] * W0
            a.append(jnp.concatenate([tile[:, :128], tile[:, 128:]], axis=0))
        b = [
            jnp.where(bit4, a[0], lane_roll(a[2], 16)),
            jnp.where(bit4, a[1], lane_roll(a[3], 16)),
            jnp.where(bit4, lane_roll(a[0], -16), a[2]),
            jnp.where(bit4, lane_roll(a[1], -16), a[3]),
        ]
        d = [
            jnp.where(bit3, b[0], lane_roll(b[1], 8)),
            jnp.where(bit3, lane_roll(b[0], -8), b[1]),
            jnp.where(bit3, b[2], lane_roll(b[3], 8)),
            jnp.where(bit3, lane_roll(b[2], -8), b[3]),
        ]
        out.append(jnp.concatenate(d, axis=0))
    return out


def z_slots(count):
    for j in range(count):
        for v in range(8):
            yield j, v, v % 2, 2 * (count * (v // 2) + j) + 1


def pack_z(fields, rows):
    shape = (rows, 128)
    lane = iota(shape, 1) & 31
    packed = [jnp.zeros(shape, F32)] * 2
    for j, v, u, s in z_slots(len(fields)):
        mine = (lane == s) | (lane == s - 1)
        packed[u] = jnp.where(mine, lane_roll(fields[j][rows * v : rows * v + rows], s), packed[u])
    return packed


def unpack_z(packed, count, rows):
    above = [[None] * 8 for _ in range(count)]
    below = [[None] * 8 for _ in range(count)]
    for j, v, u, s in z_slots(count):
        above[j][v] = lane_roll(packed[u], 31 - s)
        below[j][v] = lane_roll(packed[u], 97 - s)
    return (
        [jnp.concatenate(x, axis=0) for x in above],
        [jnp.concatenate(x, axis=0) for x in below],
    )


def grad_z(field, above, below):
    z = iota(field.shape, 1) & 31
    higher = jnp.where(z == 31, above, lane_roll(field, -1))
    lower = jnp.where(z == 0, below, lane_roll(field, 1))
    return 0.5 * (higher - lower)


def pack_y(field, rows):
    lower = iota((rows, 128), 1) < 64
    return jnp.where(lower, field[:rows], field[7 * rows :])


def grad_y(field, ghost, rows):
    lane = iota(field.shape, 1)
    moved = lane_roll(field, -32)
    following = jnp.concatenate([moved[rows:], lane_roll(ghost, -32)], axis=0)
    higher = jnp.where(lane < 96, moved, following)
    moved = lane_roll(field, 32)
    previous = jnp.concatenate([lane_roll(ghost, 32), moved[:-rows]], axis=0)
    lower = jnp.where(lane >= 32, moved, previous)
    return 0.5 * (higher - lower)


def halves(field):
    grouped = field.reshape(8, 2, 8, 128)
    return grouped[:, 0], grouped[:, 1]


def pack_x(fields, member):
    groups = []
    for field in fields:
        low, high = halves(field)
        at_end = jnp.full(low.shape, member, jnp.int32) == MEMBERS - 1
        first = jnp.where(at_end, high, low)
        last = jnp.where(at_end, low, high)
        row = iota((2, 8, 128), 1)
        packed = jnp.zeros((2, 8, 128), F32)
        for s in range(4):
            a = pltpu.roll(first[2 * s : 2 * s + 2], 7 - s, 1)
            b = pltpu.roll(last[2 * s : 2 * s + 2], s + 1, 1)
            packed = jnp.where(row == 7 - s, a, jnp.where(row == s, b, packed))
        groups.append(packed)
    return groups


def unpack_x(packed):
    above = jnp.concatenate([packed if s == 0 else pltpu.roll(packed, s, 1) for s in range(4)], axis=0)
    below = jnp.concatenate([packed if s == 0 else pltpu.roll(packed, 8 - s, 1) for s in range(4)], axis=0)
    return above, below


def grad_x(field, packed, member, own_only):
    low, high = halves(field)
    above, below = unpack_x(packed)
    row = iota(low.shape, 1)
    device = jnp.full(low.shape, member, jnp.int32)
    first = device == 0
    last = device == MEMBERS - 1
    moved_low = pltpu.roll(low, 7, 1)
    moved_high = pltpu.roll(high, 7, 1)
    up_low = jnp.where(row == 7, jnp.where(last, above, moved_high), moved_low)
    back_low = pltpu.roll(low, 1, 1)
    back_high = pltpu.roll(high, 1, 1)
    down_low = jnp.where(row == 0, jnp.where(first, below, back_high), back_low)
    own = 0.5 * (up_low - down_low)
    if own_only:
        return own.reshape(64, 128)
    up_high = jnp.where(row == 7, jnp.where(first, above, moved_low), moved_high)
    down_high = jnp.where(row == 0, jnp.where(last, below, back_low), back_high)
    other = 0.5 * (up_high - down_high)
    return jnp.stack([own, other], axis=1).reshape(128, 128)


def own_rows(field):
    return halves(field)[0].reshape(64, 128)


def kernel(patches, src_hbm, off_hbm, cnt_hbm, nb_hbm, vort_hbm, out_ref,
           src_ref, off_ref, cnt_ref, nb_ref, vort_ref,
           gbuf, wz_ref, wy_ref, lx_ref, rbuf, acc, pbuf, vbuf,
           isem, xsend, msend, csend, grecv, psend, precv, vsend, vrecv):
    patch = lax.axis_index("patch")
    member = lax.axis_index("comp")
    odd = lax.rem(patch, 2)
    mate = patch + 1 - 2 * odd
    cross = lax.rem(patch + patches - 1 + 2 * odd, patches)
    places = (patch, mate, cross)

    def chunk(position, step):
        return gbuf.at[position, pl.ds(SLOT[step % MEMBERS] * CHUNK, CHUNK)]

    def other(step):
        return lax.rem(member + step, MEMBERS)

    barrier = pltpu.get_barrier_semaphore()
    partners = (
        [(cross, member)] + [(patch, other(step)) for step in STEPS[1:]] + [(mate, member)]
    )
    for partner in partners:
        pl.semaphore_signal(barrier, inc=1, device_id=partner, device_id_type=MESH_ID)

    inputs = ((vort_hbm, vort_ref), (src_hbm, src_ref), (off_hbm, off_ref), (cnt_hbm, cnt_ref), (nb_hbm, nb_ref))
    loads = [pltpu.make_async_copy(a, b, isem.at[n]) for n, (a, b) in enumerate(inputs)]
    for load in loads:
        load.start()
    loads[0].wait()
    cells = [vort_ref[0, i].astype(F32) for i in range(COMPONENTS)]
    staged = jnp.concatenate(
        [cells[i][:, TILE * q : TILE * q + TILE] for q in range(4) for i in range(COMPONENTS)], axis=0
    ).astype(BF16)
    gbuf[0, :CHUNK, :] = staged
    pl.semaphore_wait(barrier, len(partners))

    def send(position, step, target, place, landing, send_sem):
        return pltpu.make_async_remote_copy(
            src_ref=chunk(position, step), dst_ref=chunk(place, landing),
            send_sem=send_sem, recv_sem=grecv.at[place * MEMBERS + SLOT[landing % MEMBERS]],
            device_id=target, device_id_type=MESH_ID,
        )

    def across(step):
        return send(0, 0, (patch, other(step)), 0, -step, xsend.at[step - 1])

    def to_mate(step):
        return send(0, step, (mate, member), 1, step, msend.at[step])

    def to_cross(step):
        return send(0, step, (cross, member), 2, step, csend.at[step])

    def opposite():
        return send(2, 0, (patch, other(2)), 2, 2, csend.at[2])

    def arrived(position, step):
        pltpu.make_async_remote_copy(
            src_ref=chunk(position, step), dst_ref=chunk(position, step),
            send_sem=xsend.at[0], recv_sem=grecv.at[position * MEMBERS + SLOT[step]],
            device_id=(cross, member), device_id_type=MESH_ID,
        ).wait_recv()

    started = []

    def start(copy):
        copy.start()
        started.append(copy)

    for copy in (across(1), across(3), to_cross(0), to_mate(0), across(2)):
        start(copy)
    for load in loads[1:]:
        load.wait()

    def tables(position):
        shifts, live = slot_of(places[position], src_ref, off_ref, cnt_ref)
        write_tables(position, shifts, live, member, wz_ref, wy_ref, lx_ref)

    def products(position, waiting, first):
        rows = len(STEPS) // PARTS[position]
        for part in range(PARTS[position]):
            for step in STEPS[part * rows : part * rows + rows]:
                if step in waiting:
                    arrived(position, step)
            zy_products(position, part, gbuf, wz_ref, wy_ref, rbuf)
        x_products(position, lx_ref, rbuf, acc, first)

    tables(0)
    for step in (1, 3):
        arrived(0, step)
        start(to_cross(step))
        start(to_mate(step))
    arrived(2, 0)
    start(opposite())
    arrived(0, 2)
    start(to_mate(2))
    tables(1)
    tables(2)
    products(0, (), True)
    products(1, STEPS, False)
    products(2, STEPS[1:], False)

    def exchange(buffer, send, recv):
        copies = []
        for step, place in ((1, 2), (0, 1)):
            copies.append(pltpu.make_async_remote_copy(
                src_ref=buffer.at[0], dst_ref=buffer.at[place],
                send_sem=send.at[step], recv_sem=recv.at[step],
                device_id=(places[place], member), device_id_type=MESH_ID,
            ))
        for copy in copies:
            copy.start()
        return copies

    def pick(buffer, face, index, shape):
        source = jnp.full(shape, nb_ref[0, face], jnp.int32)
        parts = [buffer[place, index].reshape(shape) for place in range(3)]
        chosen = jnp.where(source == patch, parts[0], jnp.where(source == mate, parts[1], parts[2]))
        return jnp.where(source < 0, 0.0, chosen)

    def ghosts(buffer, rows, z_count, y_count, x_count):
        shape = (rows, 128)
        groups = rows // 8
        lane = iota(shape, 1)
        zs, ys, xs = [], [], []
        for u in range(2):
            index = pl.ds(u * groups, groups)
            zs.append(jnp.where((lane & 1) == 1, pick(buffer, 5, index, shape), pick(buffer, 4, index, shape)))
        at = 2 * groups
        for j in range(y_count):
            index = pl.ds(at, groups)
            ys.append(jnp.where(lane < 64, pick(buffer, 3, index, shape), pick(buffer, 2, index, shape)))
            at += groups
        shape = (2, 8, 128)
        row = iota(shape, 1)
        for j in range(x_count):
            index = pl.ds(at, 2)
            xs.append(jnp.where(row < 4, pick(buffer, 0, index, shape), pick(buffer, 1, index, shape)))
            at += 2
        return zs, ys, xs

    px, py, pz = potential_of(acc)
    packs = pack_z([px, py], HALO) + [pack_y(px, HALO), pack_y(pz, HALO)]
    for index, part in enumerate(packs):
        pbuf[0, 2 * index : 2 * index + 2] = part.reshape(2, 8, 128)
    for index, part in enumerate(pack_x([py, pz], member)):
        pbuf[0, 8 + 2 * index : 10 + 2 * index] = part
    copies = exchange(pbuf, psend, precv)
    for copy in copies:
        copy.wait_recv()
    zs, ys, xs = ghosts(pbuf, HALO, 2, 2, 2)
    above, below = unpack_z(zs, 2, HALO)
    vx = grad_y(pz, ys[1], HALO) - grad_z(py, above[1], below[1])
    vy = grad_z(px, above[0], below[0]) - grad_x(pz, xs[1], member, False)
    vz = grad_x(py, xs[0], member, False) - grad_y(px, ys[0], HALO)
    velocity = [vx, vy, vz]
    own = [own_rows(v) for v in velocity]
    packs = pack_z(own, 8) + [pack_y(v, 8) for v in own]
    for index, part in enumerate(packs):
        vbuf[0, index] = part
    for index, part in enumerate(pack_x(velocity, member)):
        vbuf[0, 5 + 2 * index : 7 + 2 * index] = part
    vcopies = exchange(vbuf, vsend, vrecv)
    for i in range(COMPONENTS):
        for v in range(8):
            out_ref[0, i, :, 128 * v : 128 * v + 128] = own[i][8 * v : 8 * v + 8]
    for copy in vcopies:
        copy.wait_recv()
    zs, ys, xs = ghosts(vbuf, 8, 3, 3, 3)
    above, below = unpack_z(zs, 3, 8)
    spin = [
        jnp.concatenate([vort_ref[0, i, :, 128 * v : 128 * v + 128].astype(F32) for v in range(8)], axis=0)
        for i in range(COMPONENTS)
    ]
    for i in range(COMPONENTS):
        total = (
            spin[0] * grad_x(velocity[i], xs[i], member, True)
            + spin[1] * grad_y(own[i], ys[i], 8)
            + spin[2] * grad_z(own[i], above[i], below[i])
        )
        for v in range(8):
            out_ref[0, 3 + i, :, 128 * v : 128 * v + 128] = total[8 * v : 8 * v + 8]

    for copy in started + copies + vcopies:
        copy.wait_send()


def body(patches, vorticity, pair_source, pair_offset, pair_count, neighbours):
    hbm = pl.BlockSpec(memory_space=pltpu.HBM)
    vmem = pl.BlockSpec(memory_space=pltpu.VMEM)
    out = jax.ShapeDtypeStruct((1, 2 * COMPONENTS, SLAB, CELL * CELL), F32)
    both = pl.pallas_call(
        functools.partial(kernel, patches),
        out_shape=out,
        in_specs=[hbm] * 5,
        out_specs=vmem,
        scratch_shapes=[
            pltpu.SMEM((1, NEAR), jnp.int32),
            pltpu.SMEM((1, NEAR), jnp.int32),
            pltpu.SMEM((1,), jnp.int32),
            pltpu.SMEM((1, 6), jnp.int32),
            pltpu.VMEM((1, COMPONENTS, SLAB, CELL * CELL), BF16),
            pltpu.VMEM((3, PATCH_ROWS, TILE), BF16),
            pltpu.VMEM((3 * TERMS, TILE, TILE), BF16),
            pltpu.VMEM((3 * TERMS, TILE, TILE), BF16),
            pltpu.VMEM((3, HALO, 128), BF16),
            pltpu.VMEM((12, 128, TILE), BF16),
            pltpu.VMEM((12, HALO, TILE), F32),
            pltpu.VMEM((3, 12, 8, 128), F32),
            pltpu.VMEM((3, 11, 8, 128), F32),
            pltpu.SemaphoreType.DMA((5,)),
            pltpu.SemaphoreType.DMA((3,)),
            pltpu.SemaphoreType.DMA((MEMBERS,)),
            pltpu.SemaphoreType.DMA((2 * MEMBERS,)),
            pltpu.SemaphoreType.DMA((3 * MEMBERS,)),
            pltpu.SemaphoreType.DMA((2,)),
            pltpu.SemaphoreType.DMA((2,)),
            pltpu.SemaphoreType.DMA((2,)),
            pltpu.SemaphoreType.DMA((2,)),
        ],
        compiler_params=pltpu.CompilerParams(
            collective_id=0, has_side_effects=True, vmem_limit_bytes=40 << 20
        ),
    )(pair_source, pair_offset, pair_count, neighbours, vorticity)
    return both[:, :3], both[:, 3:]


def solution(mesh):
    return jax.shard_map(
        functools.partial(body, mesh.shape["patch"]),
        mesh=mesh,
        in_specs=(
            P("patch", None, "comp", None),
            P("patch", None),
            P("patch", None),
            P("patch"),
            P("patch", None),
        ),
        out_specs=(P("patch", None, "comp", None), P("patch", None, "comp", None)),
        check_vma=False,
    )
```

```python
import functools

import jax
import jax.numpy as jnp
from jax import lax
from jax.experimental import pallas as pl
from jax.experimental.pallas import tpu as pltpu
from jax.sharding import PartitionSpec as P

CELL = 32
TERMS = 4
NEAR = 3
MEMBERS = 4
SLAB = CELL // MEMBERS
COMPONENTS = 3
CHUNK = 4 * COMPONENTS * SLAB
PATCH_ROWS = MEMBERS * CHUNK
TILE = 256
HALO = 16
W0 = 0.08 / 0.75 ** 0.5
F32 = jnp.float32
BF16 = jnp.bfloat16
MESH_ID = pl.DeviceIdType.MESH
STEPS = (0, 1, 3, 2)
SLOT = {step: slot for slot, step in enumerate(STEPS)}
PIECES = 1
PARTS = (1, 1, 2)


def iota(shape, dim):
    return lax.broadcasted_iota(jnp.int32, shape, dim)


def lane_roll(values, shift):
    shift = shift % 128
    return values if shift == 0 else pltpu.roll(values, shift, values.ndim - 1)


def row_roll(values, shift):
    shift = shift % 8
    if shift == 0:
        return values
    grouped = values.reshape(-1, 8, 128)
    return pltpu.roll(grouped, shift, 1).reshape(values.shape)


def slot_of(source, src_ref, off_ref, cnt_ref):
    code = jnp.int32(13)
    live = jnp.int32(0)
    count = cnt_ref[0]
    for j in range(NEAR):
        hit = (count > j) & (src_ref[0, j] == source)
        code = jnp.where(hit, off_ref[0, j], code)
        live = jnp.where(hit, 1, live)
    shifts = (lax.div(code, 9) - 1, lax.rem(lax.div(code, 3), 3) - 1, lax.rem(code, 3) - 1)
    return shifts, live


def gauss(spacing, scale):
    spacing = spacing.astype(F32)
    return jnp.exp(-(spacing * spacing / 1.125) * scale)


def write_tables(position, shifts, live, member, wz_ref, wy_ref, lx_ref):
    shift_x, shift_y, shift_z = shifts
    rows = iota((CELL, TILE), 0)
    cols = iota((CELL, TILE), 1)
    gap_z = (cols >> 3) - rows - CELL * shift_z
    gap_y = ((cols >> 5) + 8 * ((cols >> 3) & 3)) - rows - CELL * shift_y
    low = cols & 7
    low8 = iota((8, TILE), 1) & 7
    for k in range(TERMS):
        scale = 1.0 / 16.0 ** k
        table = gauss(gap_z, scale)
        wz_ref[position * TERMS + k] = jnp.concatenate(
            [jnp.where(low == y, table, 0.0) for y in range(8)], axis=0
        ).astype(BF16)
        table = gauss(gap_y, scale)
        wy_ref[position * TERMS + k] = jnp.concatenate(
            [jnp.where(low8 == z, table[8 * h : 8 * h + 8], 0.0) for h in range(4) for z in range(8)],
            axis=0,
        ).astype(BF16)
    row = iota((HALO, 128), 0)
    col = iota((HALO, 128), 1)
    plane = (SLAB * member + jnp.where(row < 12, row, row - HALO)) & (CELL - 1)
    if PARTS[position] == 1:
        term = col >> 5
        slot = (col >> 3) & 3
    else:
        term = (col >> 4) & 3
        slot = 2 * (col >> 6) + ((col >> 3) & 1)
    step = slot ^ (slot >> 1)
    source = SLAB * ((member + step) & 3) + (col & 7)
    scale = jnp.where(term == 0, 1.0, jnp.where(term == 1, 1 / 16, jnp.where(term == 2, 1 / 256, 1 / 4096)))
    weight = jnp.where(term == 0, 1.0, jnp.where(term == 1, 0.5, jnp.where(term == 2, 0.25, 0.125)))
    table = gauss(plane - source - CELL * shift_x, scale).astype(BF16).astype(F32)
    lx_ref[position] = (table * weight * live.astype(F32)).astype(BF16)


def zy_products(position, part, gbuf, wz_ref, wy_ref, rbuf):
    slots = MEMBERS // PARTS[position]
    rows = slots * CHUNK
    lower = iota((slots, 24, 128), 2) < 64
    for k in range(TERMS):
        along_z = jnp.dot(
            gbuf[position, part * rows : part * rows + rows],
            wz_ref[position * TERMS + k],
            preferred_element_type=F32,
        ).reshape(slots, 4, 24, TILE)
        blocks = [[None] * 2 for _ in range(4)]
        for pair in range(2):
            for half in range(2):
                a = along_z[:, 2 * pair, :, 128 * half : 128 * half + 128]
                b = along_z[:, 2 * pair + 1, :, 128 * half : 128 * half + 128]
                blocks[2 * half][pair] = jnp.where(lower, a, lane_roll(b, 64))
                blocks[2 * half + 1][pair] = jnp.where(lower, lane_roll(a, 64), b)
        pieces = []
        for block in blocks:
            joined = jnp.concatenate(block, axis=2)
            for i in range(COMPONENTS):
                pieces.append(joined[:, 8 * i : 8 * i + 8].reshape(8 * slots, TILE))
        swapped = jnp.concatenate(pieces, axis=0).astype(BF16)
        along_y = jnp.dot(swapped, wy_ref[position * TERMS + k], preferred_element_type=F32).astype(BF16)
        at = (part * TERMS + k) * 8 * slots
        rbuf[:, at : at + 8 * slots, :] = along_y.reshape(12, 8 * slots, TILE)


def x_products(position, lx_ref, rbuf, acc, first):
    for block in range(12):
        term = jnp.dot(lx_ref[position], rbuf[block], preferred_element_type=F32)
        acc[block] = term if first else acc[block] + term


def potential_of(acc):
    lane = iota((2 * HALO, 128), 1)
    bit4 = (lane & 16) == 0
    bit3 = (lane & 8) == 0
    out = []
    for i in range(COMPONENTS):
        a = []
        for block in range(4):
            tile = acc[3 * block + i] * W0
            a.append(jnp.concatenate([tile[:, :128], tile[:, 128:]], axis=0))
        b = [
            jnp.where(bit4, a[0], lane_roll(a[2], 16)),
            jnp.where(bit4, a[1], lane_roll(a[3], 16)),
            jnp.where(bit4, lane_roll(a[0], -16), a[2]),
            jnp.where(bit4, lane_roll(a[1], -16), a[3]),
        ]
        d = [
            jnp.where(bit3, b[0], lane_roll(b[1], 8)),
            jnp.where(bit3, lane_roll(b[0], -8), b[1]),
            jnp.where(bit3, b[2], lane_roll(b[3], 8)),
            jnp.where(bit3, lane_roll(b[2], -8), b[3]),
        ]
        out.append(jnp.concatenate(d, axis=0))
    return out


def z_slots(count):
    for j in range(count):
        for v in range(8):
            yield j, v, v % 2, 2 * (count * (v // 2) + j) + 1


def pack_z(fields, rows):
    shape = (rows, 128)
    lane = iota(shape, 1) & 31
    packed = [jnp.zeros(shape, F32)] * 2
    for j, v, u, s in z_slots(len(fields)):
        mine = (lane == s) | (lane == s - 1)
        packed[u] = jnp.where(mine, lane_roll(fields[j][rows * v : rows * v + rows], s), packed[u])
    return packed


def unpack_z(packed, count, rows):
    above = [[None] * 8 for _ in range(count)]
    below = [[None] * 8 for _ in range(count)]
    for j, v, u, s in z_slots(count):
        above[j][v] = lane_roll(packed[u], 31 - s)
        below[j][v] = lane_roll(packed[u], 97 - s)
    return (
        [jnp.concatenate(x, axis=0) for x in above],
        [jnp.concatenate(x, axis=0) for x in below],
    )


def grad_z(field, above, below):
    z = iota(field.shape, 1) & 31
    higher = jnp.where(z == 31, above, lane_roll(field, -1))
    lower = jnp.where(z == 0, below, lane_roll(field, 1))
    return 0.5 * (higher - lower)


def pack_y(field, rows):
    lower = iota((rows, 128), 1) < 64
    return jnp.where(lower, field[:rows], field[7 * rows :])


def grad_y(field, ghost, rows):
    lane = iota(field.shape, 1)
    moved = lane_roll(field, -32)
    following = jnp.concatenate([moved[rows:], lane_roll(ghost, -32)], axis=0)
    higher = jnp.where(lane < 96, moved, following)
    moved = lane_roll(field, 32)
    previous = jnp.concatenate([lane_roll(ghost, 32), moved[:-rows]], axis=0)
    lower = jnp.where(lane >= 32, moved, previous)
    return 0.5 * (higher - lower)


def halves(field):
    grouped = field.reshape(8, 2, 8, 128)
    return grouped[:, 0], grouped[:, 1]


def pack_x(fields, member):
    groups = []
    for field in fields:
        low, high = halves(field)
        at_end = jnp.full(low.shape, member, jnp.int32) == MEMBERS - 1
        first = jnp.where(at_end, high, low)
        last = jnp.where(at_end, low, high)
        row = iota((2, 8, 128), 1)
        packed = jnp.zeros((2, 8, 128), F32)
        for s in range(4):
            a = pltpu.roll(first[2 * s : 2 * s + 2], 7 - s, 1)
            b = pltpu.roll(last[2 * s : 2 * s + 2], s + 1, 1)
            packed = jnp.where(row == 7 - s, a, jnp.where(row == s, b, packed))
        groups.append(packed)
    return groups


def unpack_x(packed):
    above = jnp.concatenate([packed if s == 0 else pltpu.roll(packed, s, 1) for s in range(4)], axis=0)
    below = jnp.concatenate([packed if s == 0 else pltpu.roll(packed, 8 - s, 1) for s in range(4)], axis=0)
    return above, below


def grad_x(field, packed, member, own_only):
    low, high = halves(field)
    above, below = unpack_x(packed)
    row = iota(low.shape, 1)
    device = jnp.full(low.shape, member, jnp.int32)
    first = device == 0
    last = device == MEMBERS - 1
    moved_low = pltpu.roll(low, 7, 1)
    moved_high = pltpu.roll(high, 7, 1)
    up_low = jnp.where(row == 7, jnp.where(last, above, moved_high), moved_low)
    back_low = pltpu.roll(low, 1, 1)
    back_high = pltpu.roll(high, 1, 1)
    down_low = jnp.where(row == 0, jnp.where(first, below, back_high), back_low)
    own = 0.5 * (up_low - down_low)
    if own_only:
        return own.reshape(64, 128)
    up_high = jnp.where(row == 7, jnp.where(first, above, moved_low), moved_high)
    down_high = jnp.where(row == 0, jnp.where(last, below, back_low), back_high)
    other = 0.5 * (up_high - down_high)
    return jnp.stack([own, other], axis=1).reshape(128, 128)


def own_rows(field):
    return halves(field)[0].reshape(64, 128)


def kernel(patches, src_hbm, off_hbm, cnt_hbm, nb_hbm, vort_hbm, out_ref,
           src_ref, off_ref, cnt_ref, nb_ref, vort_ref,
           gbuf, wz_ref, wy_ref, lx_ref, rbuf, acc, pbuf, vbuf,
           isem, xsend, msend, csend, grecv, psend, precv, vsend, vrecv):
    patch = lax.axis_index("patch")
    member = lax.axis_index("comp")
    odd = lax.rem(patch, 2)
    mate = patch + 1 - 2 * odd
    cross = lax.rem(patch + patches - 1 + 2 * odd, patches)
    places = (patch, mate, cross)
    inner = (patch > 0) & (patch < patches - 1)

    def chunk(position, step, piece):
        rows = CHUNK // PIECES
        return gbuf.at[position, pl.ds(SLOT[step % MEMBERS] * CHUNK + piece * rows, rows)]

    def other(step):
        return lax.rem(member + step, MEMBERS)

    barrier = pltpu.get_barrier_semaphore()

    def greet(partner):
        pl.semaphore_signal(barrier, inc=1, device_id=partner, device_id_type=MESH_ID)

    @pl.when(inner)
    def _():
        greet((cross, member))

    for step in STEPS[1:]:
        greet((patch, other(step)))
    greet((mate, member))

    inputs = ((vort_hbm, vort_ref), (src_hbm, src_ref), (off_hbm, off_ref), (cnt_hbm, cnt_ref), (nb_hbm, nb_ref))
    loads = [pltpu.make_async_copy(a, b, isem.at[n]) for n, (a, b) in enumerate(inputs)]
    for load in loads:
        load.start()
    loads[0].wait()
    cells = [vort_ref[0, i].astype(F32) for i in range(COMPONENTS)]
    staged = jnp.concatenate(
        [cells[i][:, TILE * q : TILE * q + TILE] for q in range(4) for i in range(COMPONENTS)], axis=0
    ).astype(BF16)
    gbuf[0, :CHUNK, :] = staged
    pl.semaphore_wait(barrier, jnp.where(inner, 5, 4))

    def send(position, step, piece, target, place, landing, send_sem):
        return pltpu.make_async_remote_copy(
            src_ref=chunk(position, step, piece), dst_ref=chunk(place, landing, piece),
            send_sem=send_sem, recv_sem=grecv.at[place * MEMBERS + SLOT[landing % MEMBERS], piece],
            device_id=target, device_id_type=MESH_ID,
        )

    def across(step, piece):
        return send(0, 0, piece, (patch, other(step)), 0, -step, xsend.at[step - 1, piece])

    def to_mate(step, piece):
        return send(0, step, piece, (mate, member), 1, step, msend.at[step, piece])

    def to_cross(step, piece):
        return send(0, step, piece, (cross, member), 2, step, csend.at[step, piece])

    def opposite(piece):
        return send(2, 0, piece, (patch, other(2)), 2, 2, csend.at[2, piece])

    def arrived(position, step, piece):
        pltpu.make_async_remote_copy(
            src_ref=chunk(position, step, piece), dst_ref=chunk(position, step, piece),
            send_sem=xsend.at[0, 0], recv_sem=grecv.at[position * MEMBERS + SLOT[step], piece],
            device_id=(cross, member), device_id_type=MESH_ID,
        ).wait_recv()

    pieces = range(PIECES)
    for step in (1, 3):
        for piece in pieces:
            across(step, piece).start()

    @pl.when(inner)
    def _():
        for piece in pieces:
            to_cross(0, piece).start()

    for piece in pieces:
        to_mate(0, piece).start()
    for piece in pieces:
        across(2, piece).start()
    for load in loads[1:]:
        load.wait()

    def tables(position):
        shifts, live = slot_of(places[position], src_ref, off_ref, cnt_ref)
        write_tables(position, shifts, live, member, wz_ref, wy_ref, lx_ref)

    def products(position, waiting, first):
        rows = len(STEPS) // PARTS[position]
        for part in range(PARTS[position]):
            for step in STEPS[part * rows : part * rows + rows]:
                for piece in pieces if step in waiting else ():
                    arrived(position, step, piece)
            zy_products(position, part, gbuf, wz_ref, wy_ref, rbuf)
        x_products(position, lx_ref, rbuf, acc, first)

    tables(0)
    for piece in pieces:
        for step in (1, 3):
            arrived(0, step, piece)

            @pl.when(inner)
            def _():
                to_cross(step, piece).start()

            to_mate(step, piece).start()

    @pl.when(inner)
    def _():
        for piece in pieces:
            arrived(2, 0, piece)
            opposite(piece).start()

    for piece in pieces:
        arrived(0, 2, piece)
        to_mate(2, piece).start()
    tables(1)
    tables(2)
    products(0, (), True)
    products(1, STEPS, False)

    @pl.when(inner)
    def _():
        products(2, STEPS[1:], False)

    @pl.when(jnp.logical_not(inner))
    def _():
        pbuf[2] = jnp.zeros(pbuf.shape[1:], F32)
        vbuf[2] = jnp.zeros(vbuf.shape[1:], F32)

    def exchange(buffer, send, recv):
        return [
            pltpu.make_async_remote_copy(
                src_ref=buffer.at[0], dst_ref=buffer.at[place],
                send_sem=send.at[place - 1], recv_sem=recv.at[place - 1],
                device_id=(places[place], member), device_id_type=MESH_ID,
            )
            for place in (2, 1)
        ]

    def act(copies, name):
        @pl.when(inner)
        def _():
            getattr(copies[0], name)()

        getattr(copies[1], name)()

    def pick(buffer, face, index, shape):
        source = jnp.full(shape, nb_ref[0, face], jnp.int32)
        parts = [buffer[place, index].reshape(shape) for place in range(3)]
        chosen = jnp.where(source == patch, parts[0], jnp.where(source == mate, parts[1], parts[2]))
        return jnp.where(source < 0, 0.0, chosen)

    def ghosts(buffer, rows, z_count, y_count, x_count):
        shape = (rows, 128)
        groups = rows // 8
        lane = iota(shape, 1)
        zs, ys, xs = [], [], []
        for u in range(2):
            index = pl.ds(u * groups, groups)
            zs.append(jnp.where((lane & 1) == 1, pick(buffer, 5, index, shape), pick(buffer, 4, index, shape)))
        at = 2 * groups
        for j in range(y_count):
            index = pl.ds(at, groups)
            ys.append(jnp.where(lane < 64, pick(buffer, 3, index, shape), pick(buffer, 2, index, shape)))
            at += groups
        shape = (2, 8, 128)
        row = iota(shape, 1)
        for j in range(x_count):
            index = pl.ds(at, 2)
            xs.append(jnp.where(row < 4, pick(buffer, 0, index, shape), pick(buffer, 1, index, shape)))
            at += 2
        return zs, ys, xs

    px, py, pz = potential_of(acc)
    packs = pack_z([px, py], HALO) + [pack_y(px, HALO), pack_y(pz, HALO)]
    for index, part in enumerate(packs):
        pbuf[0, 2 * index : 2 * index + 2] = part.reshape(2, 8, 128)
    for index, part in enumerate(pack_x([py, pz], member)):
        pbuf[0, 8 + 2 * index : 10 + 2 * index] = part
    copies = exchange(pbuf, psend, precv)
    act(copies, "start")
    act(copies, "wait_recv")
    zs, ys, xs = ghosts(pbuf, HALO, 2, 2, 2)
    above, below = unpack_z(zs, 2, HALO)
    vx = grad_y(pz, ys[1], HALO) - grad_z(py, above[1], below[1])
    vy = grad_z(px, above[0], below[0]) - grad_x(pz, xs[1], member, False)
    vz = grad_x(py, xs[0], member, False) - grad_y(px, ys[0], HALO)
    velocity = [vx, vy, vz]
    own = [own_rows(v) for v in velocity]
    packs = pack_z(own, 8) + [pack_y(v, 8) for v in own]
    for index, part in enumerate(packs):
        vbuf[0, index] = part
    for index, part in enumerate(pack_x(velocity, member)):
        vbuf[0, 5 + 2 * index : 7 + 2 * index] = part
    vcopies = exchange(vbuf, vsend, vrecv)
    act(vcopies, "start")
    for i in range(COMPONENTS):
        for v in range(8):
            out_ref[0, i, :, 128 * v : 128 * v + 128] = own[i][8 * v : 8 * v + 8]
    act(vcopies, "wait_recv")
    zs, ys, xs = ghosts(vbuf, 8, 3, 3, 3)
    above, below = unpack_z(zs, 3, 8)
    spin = [
        jnp.concatenate([vort_ref[0, i, :, 128 * v : 128 * v + 128].astype(F32) for v in range(8)], axis=0)
        for i in range(COMPONENTS)
    ]
    for i in range(COMPONENTS):
        total = (
            spin[0] * grad_x(velocity[i], xs[i], member, True)
            + spin[1] * grad_y(own[i], ys[i], 8)
            + spin[2] * grad_z(own[i], above[i], below[i])
        )
        for v in range(8):
            out_ref[0, 3 + i, :, 128 * v : 128 * v + 128] = total[8 * v : 8 * v + 8]

    for piece in pieces:
        for step in (1, 2, 3):
            across(step, piece).wait_send()
        for step in STEPS:
            to_mate(step, piece).wait_send()

    @pl.when(inner)
    def _():
        for piece in pieces:
            for step in (0, 1, 3):
                to_cross(step, piece).wait_send()
            opposite(piece).wait_send()

    act(copies, "wait_send")
    act(vcopies, "wait_send")


def body(patches, vorticity, pair_source, pair_offset, pair_count, neighbours):
    hbm = pl.BlockSpec(memory_space=pltpu.HBM)
    vmem = pl.BlockSpec(memory_space=pltpu.VMEM)
    out = jax.ShapeDtypeStruct((1, 2 * COMPONENTS, SLAB, CELL * CELL), F32)
    both = pl.pallas_call(
        functools.partial(kernel, patches),
        out_shape=out,
        in_specs=[hbm] * 5,
        out_specs=vmem,
        scratch_shapes=[
            pltpu.SMEM((1, NEAR), jnp.int32),
            pltpu.SMEM((1, NEAR), jnp.int32),
            pltpu.SMEM((1,), jnp.int32),
            pltpu.SMEM((1, 6), jnp.int32),
            pltpu.VMEM((1, COMPONENTS, SLAB, CELL * CELL), BF16),
            pltpu.VMEM((3, PATCH_ROWS, TILE), BF16),
            pltpu.VMEM((3 * TERMS, TILE, TILE), BF16),
            pltpu.VMEM((3 * TERMS, TILE, TILE), BF16),
            pltpu.VMEM((3, HALO, 128), BF16),
            pltpu.VMEM((12, 128, TILE), BF16),
            pltpu.VMEM((12, HALO, TILE), F32),
            pltpu.VMEM((3, 12, 8, 128), F32),
            pltpu.VMEM((3, 11, 8, 128), F32),
            pltpu.SemaphoreType.DMA((5,)),
            pltpu.SemaphoreType.DMA((3, PIECES)),
            pltpu.SemaphoreType.DMA((MEMBERS, PIECES)),
            pltpu.SemaphoreType.DMA((MEMBERS, PIECES)),
            pltpu.SemaphoreType.DMA((3 * MEMBERS, PIECES)),
            pltpu.SemaphoreType.DMA((2,)),
            pltpu.SemaphoreType.DMA((2,)),
            pltpu.SemaphoreType.DMA((2,)),
            pltpu.SemaphoreType.DMA((2,)),
        ],
        compiler_params=pltpu.CompilerParams(
            collective_id=0, has_side_effects=True, vmem_limit_bytes=40 << 20
        ),
    )(pair_source, pair_offset, pair_count, neighbours, vorticity)
    return both[:, :3], both[:, 3:]


def solution(mesh):
    return jax.shard_map(
        functools.partial(body, mesh.shape["patch"]),
        mesh=mesh,
        in_specs=(
            P("patch", None, "comp", None),
            P("patch", None),
            P("patch", None),
            P("patch"),
            P("patch", None),
        ),
        out_specs=(P("patch", None, "comp", None), P("patch", None, "comp", None)),
        check_vma=False,
    )
```

```python
import functools

import jax
import jax.numpy as jnp
from jax import lax
from jax.experimental import pallas as pl
from jax.experimental.pallas import tpu as pltpu
from jax.sharding import PartitionSpec as P

CELL = 32
TERMS = 4
NEAR = 3
MEMBERS = 4
SLAB = CELL // MEMBERS
COMPONENTS = 3
CHUNK = 4 * COMPONENTS * SLAB
PATCH_ROWS = MEMBERS * CHUNK
TILE = 256
HALO = 16
W0 = 0.08 / 0.75 ** 0.5
F32 = jnp.float32
BF16 = jnp.bfloat16
MESH_ID = pl.DeviceIdType.MESH
STEPS = (0, 1, 3, 2)
SLOT = {step: slot for slot, step in enumerate(STEPS)}
PIECES = 1
OWN, MATE, FAR, BACK = range(4)
SOURCES = (OWN, MATE, FAR, OWN)
PARTS = (2, 1, 2, 1)


def iota(shape, dim):
    return lax.broadcasted_iota(jnp.int32, shape, dim)


def lane_roll(values, shift):
    shift = shift % 128
    return values if shift == 0 else pltpu.roll(values, shift, values.ndim - 1)


def row_roll(values, shift):
    shift = shift % 8
    if shift == 0:
        return values
    grouped = values.reshape(-1, 8, 128)
    return pltpu.roll(grouped, shift, 1).reshape(values.shape)


def slot_of(source, src_ref, off_ref, cnt_ref):
    code = jnp.int32(13)
    live = jnp.int32(0)
    count = cnt_ref[0]
    for j in range(NEAR):
        hit = (count > j) & (src_ref[0, j] == source)
        code = jnp.where(hit, off_ref[0, j], code)
        live = jnp.where(hit, 1, live)
    shifts = (lax.div(code, 9) - 1, lax.rem(lax.div(code, 3), 3) - 1, lax.rem(code, 3) - 1)
    return shifts, live


def gauss(spacing, scale):
    spacing = spacing.astype(F32)
    return jnp.exp(-(spacing * spacing / 1.125) * scale)


def write_tables(position, shifts, live, member, wz_ref, wy_ref, lx_ref):
    shift_x, shift_y, shift_z = shifts
    rows = iota((CELL, TILE), 0)
    cols = iota((CELL, TILE), 1)
    gap_z = (cols >> 3) - rows - CELL * shift_z
    gap_y = ((cols >> 5) + 8 * ((cols >> 3) & 3)) - rows - CELL * shift_y
    low = cols & 7
    low8 = iota((8, TILE), 1) & 7
    for k in range(TERMS):
        scale = 1.0 / 16.0 ** k
        table = gauss(gap_z, scale)
        wz_ref[position * TERMS + k] = jnp.concatenate(
            [jnp.where(low == y, table, 0.0) for y in range(8)], axis=0
        ).astype(BF16)
        table = gauss(gap_y, scale)
        wy_ref[position * TERMS + k] = jnp.concatenate(
            [jnp.where(low8 == z, table[8 * h : 8 * h + 8], 0.0) for h in range(4) for z in range(8)],
            axis=0,
        ).astype(BF16)
    row = iota((HALO, 128), 0)
    col = iota((HALO, 128), 1)
    plane = (SLAB * member + jnp.where(row < 12, row, row - HALO)) & (CELL - 1)
    if PARTS[position] == 1:
        term = col >> 5
        slot = (col >> 3) & 3
    else:
        term = (col >> 4) & 3
        slot = 2 * (col >> 6) + ((col >> 3) & 1)
    step = slot ^ (slot >> 1)
    source = SLAB * ((member + step) & 3) + (col & 7)
    scale = jnp.where(term == 0, 1.0, jnp.where(term == 1, 1 / 16, jnp.where(term == 2, 1 / 256, 1 / 4096)))
    weight = jnp.where(term == 0, 1.0, jnp.where(term == 1, 0.5, jnp.where(term == 2, 0.25, 0.125)))
    table = gauss(plane - source - CELL * shift_x, scale).astype(BF16).astype(F32)
    lx_ref[position] = (table * weight * live).astype(BF16)


def zy_products(position, part, gbuf, wz_ref, wy_ref, rbuf):
    slots = MEMBERS // PARTS[position]
    rows = slots * CHUNK
    lower = iota((slots, 24, 128), 2) < 64
    for k in range(TERMS):
        along_z = jnp.dot(
            gbuf[SOURCES[position], part * rows : part * rows + rows],
            wz_ref[position * TERMS + k],
            preferred_element_type=F32,
        ).reshape(slots, 4, 24, TILE)
        blocks = [[None] * 2 for _ in range(4)]
        for pair in range(2):
            for half in range(2):
                a = along_z[:, 2 * pair, :, 128 * half : 128 * half + 128]
                b = along_z[:, 2 * pair + 1, :, 128 * half : 128 * half + 128]
                blocks[2 * half][pair] = jnp.where(lower, a, lane_roll(b, 64))
                blocks[2 * half + 1][pair] = jnp.where(lower, lane_roll(a, 64), b)
        pieces = []
        for block in blocks:
            joined = jnp.concatenate(block, axis=2)
            for i in range(COMPONENTS):
                pieces.append(joined[:, 8 * i : 8 * i + 8].reshape(8 * slots, TILE))
        swapped = jnp.concatenate(pieces, axis=0).astype(BF16)
        along_y = jnp.dot(swapped, wy_ref[position * TERMS + k], preferred_element_type=F32).astype(BF16)
        at = (part * TERMS + k) * 8 * slots
        rbuf[:, at : at + 8 * slots, :] = along_y.reshape(12, 8 * slots, TILE)


def x_products(position, total, lx_ref, rbuf, acc, first):
    for block in range(12):
        term = jnp.dot(lx_ref[position], rbuf[block], preferred_element_type=F32)
        acc[total, block] = term if first else acc[total, block] + term


def potential_of(acc, total):
    lane = iota((2 * HALO, 128), 1)
    bit4 = (lane & 16) == 0
    bit3 = (lane & 8) == 0
    out = []
    for i in range(COMPONENTS):
        a = []
        for block in range(4):
            tile = acc[total, 3 * block + i] * W0
            a.append(jnp.concatenate([tile[:, :128], tile[:, 128:]], axis=0))
        b = [
            jnp.where(bit4, a[0], lane_roll(a[2], 16)),
            jnp.where(bit4, a[1], lane_roll(a[3], 16)),
            jnp.where(bit4, lane_roll(a[0], -16), a[2]),
            jnp.where(bit4, lane_roll(a[1], -16), a[3]),
        ]
        d = [
            jnp.where(bit3, b[0], lane_roll(b[1], 8)),
            jnp.where(bit3, lane_roll(b[0], -8), b[1]),
            jnp.where(bit3, b[2], lane_roll(b[3], 8)),
            jnp.where(bit3, lane_roll(b[2], -8), b[3]),
        ]
        out.append(jnp.concatenate(d, axis=0))
    return out


def z_slots(count):
    for j in range(count):
        for v in range(8):
            yield j, v, v % 2, 2 * (count * (v // 2) + j) + 1


def pack_z(fields, rows):
    shape = (rows, 128)
    lane = iota(shape, 1) & 31
    packed = [jnp.zeros(shape, F32)] * 2
    for j, v, u, s in z_slots(len(fields)):
        mine = (lane == s) | (lane == s - 1)
        packed[u] = jnp.where(mine, lane_roll(fields[j][rows * v : rows * v + rows], s), packed[u])
    return packed


def unpack_z(packed, count, rows):
    above = [[None] * 8 for _ in range(count)]
    below = [[None] * 8 for _ in range(count)]
    for j, v, u, s in z_slots(count):
        above[j][v] = lane_roll(packed[u], 31 - s)
        below[j][v] = lane_roll(packed[u], 97 - s)
    return (
        [jnp.concatenate(x, axis=0) for x in above],
        [jnp.concatenate(x, axis=0) for x in below],
    )


def grad_z(field, above, below):
    z = iota(field.shape, 1) & 31
    higher = jnp.where(z == 31, above, lane_roll(field, -1))
    lower = jnp.where(z == 0, below, lane_roll(field, 1))
    return 0.5 * (higher - lower)


def pack_y(field, rows):
    lower = iota((rows, 128), 1) < 64
    return jnp.where(lower, field[:rows], field[7 * rows :])


def grad_y(field, ghost, rows):
    lane = iota(field.shape, 1)
    moved = lane_roll(field, -32)
    following = jnp.concatenate([moved[rows:], lane_roll(ghost, -32)], axis=0)
    higher = jnp.where(lane < 96, moved, following)
    moved = lane_roll(field, 32)
    previous = jnp.concatenate([lane_roll(ghost, 32), moved[:-rows]], axis=0)
    lower = jnp.where(lane >= 32, moved, previous)
    return 0.5 * (higher - lower)


def halves(field):
    grouped = field.reshape(8, 2, 8, 128)
    return grouped[:, 0], grouped[:, 1]


def pack_x(fields, member):
    groups = []
    for field in fields:
        low, high = halves(field)
        at_end = jnp.full(low.shape, member, jnp.int32) == MEMBERS - 1
        first = jnp.where(at_end, high, low)
        last = jnp.where(at_end, low, high)
        row = iota((2, 8, 128), 1)
        packed = jnp.zeros((2, 8, 128), F32)
        for s in range(4):
            a = pltpu.roll(first[2 * s : 2 * s + 2], 7 - s, 1)
            b = pltpu.roll(last[2 * s : 2 * s + 2], s + 1, 1)
            packed = jnp.where(row == 7 - s, a, jnp.where(row == s, b, packed))
        groups.append(packed)
    return groups


def unpack_x(packed):
    above = jnp.concatenate([packed if s == 0 else pltpu.roll(packed, s, 1) for s in range(4)], axis=0)
    below = jnp.concatenate([packed if s == 0 else pltpu.roll(packed, 8 - s, 1) for s in range(4)], axis=0)
    return above, below


def grad_x(field, packed, member, own_only):
    low, high = halves(field)
    above, below = unpack_x(packed)
    row = iota(low.shape, 1)
    device = jnp.full(low.shape, member, jnp.int32)
    first = device == 0
    last = device == MEMBERS - 1
    moved_low = pltpu.roll(low, 7, 1)
    moved_high = pltpu.roll(high, 7, 1)
    up_low = jnp.where(row == 7, jnp.where(last, above, moved_high), moved_low)
    back_low = pltpu.roll(low, 1, 1)
    back_high = pltpu.roll(high, 1, 1)
    down_low = jnp.where(row == 0, jnp.where(first, below, back_high), back_low)
    own = 0.5 * (up_low - down_low)
    if own_only:
        return own.reshape(64, 128)
    up_high = jnp.where(row == 7, jnp.where(first, above, moved_low), moved_high)
    down_high = jnp.where(row == 0, jnp.where(last, below, back_low), back_high)
    other = 0.5 * (up_high - down_high)
    return jnp.stack([own, other], axis=1).reshape(128, 128)


def own_rows(field):
    return halves(field)[0].reshape(64, 128)


def kernel(patches, src_hbm, off_hbm, cnt_hbm, nb_hbm, vort_hbm, out_ref,
           src_ref, off_ref, cnt_ref, nb_ref, vort_ref,
           gbuf, wz_ref, wy_ref, lx_ref, rbuf, acc, potential, pbuf, back, vbuf, info,
           isem, xsend, msend, csend, grecv, psend, precv, vsend, vrecv, nsend, nrecv):
    patch = lax.axis_index("patch")
    member = lax.axis_index("comp")
    odd = lax.rem(patch, 2)
    mate = patch + 1 - 2 * odd
    cross = lax.rem(patch + patches - 1 + 2 * odd, patches)
    places = (patch, mate, cross)
    inner = (patch > 0) & (patch < patches - 1)

    def chunk(position, step, piece):
        rows = CHUNK // PIECES
        return gbuf.at[position, pl.ds(SLOT[step % MEMBERS] * CHUNK + piece * rows, rows)]

    def other(step):
        return lax.rem(member + step, MEMBERS)

    barrier = pltpu.get_barrier_semaphore()

    def greet(partner):
        pl.semaphore_signal(barrier, inc=1, device_id=partner, device_id_type=MESH_ID)

    @pl.when(inner)
    def _():
        greet((cross, member))

    for step in STEPS[1:]:
        greet((patch, other(step)))
    greet((mate, member))

    inputs = ((vort_hbm, vort_ref), (src_hbm, src_ref), (off_hbm, off_ref), (cnt_hbm, cnt_ref), (nb_hbm, nb_ref))
    loads = [pltpu.make_async_copy(a, b, isem.at[n]) for n, (a, b) in enumerate(inputs)]
    for load in loads:
        load.start()
    loads[0].wait()
    cells = [vort_ref[0, i].astype(F32) for i in range(COMPONENTS)]
    staged = jnp.concatenate(
        [cells[i][:, TILE * q : TILE * q + TILE] for q in range(4) for i in range(COMPONENTS)], axis=0
    ).astype(BF16)
    gbuf[0, :CHUNK, :] = staged
    pl.semaphore_wait(barrier, jnp.where(inner, 5, 4))

    def send(position, step, piece, target, place, landing, send_sem):
        return pltpu.make_async_remote_copy(
            src_ref=chunk(position, step, piece), dst_ref=chunk(place, landing, piece),
            send_sem=send_sem, recv_sem=grecv.at[place * MEMBERS + SLOT[landing % MEMBERS], piece],
            device_id=target, device_id_type=MESH_ID,
        )

    def across(step, piece):
        return send(0, 0, piece, (patch, other(step)), 0, -step, xsend.at[step - 1, piece])

    def to_mate(step, piece):
        return send(0, step, piece, (mate, member), 1, step, msend.at[step, piece])

    def to_cross(step, piece):
        return send(0, step, piece, (cross, member), 2, step, csend.at[step, piece])

    def opposite(piece):
        return send(2, 0, piece, (patch, other(2)), 2, 2, csend.at[2, piece])

    def arrived(position, step, piece):
        pltpu.make_async_remote_copy(
            src_ref=chunk(position, step, piece), dst_ref=chunk(position, step, piece),
            send_sem=xsend.at[0, 0], recv_sem=grecv.at[position * MEMBERS + SLOT[step], piece],
            device_id=(cross, member), device_id_type=MESH_ID,
        ).wait_recv()

    pieces = range(PIECES)
    for step in (1, 3):
        for piece in pieces:
            across(step, piece).start()

    @pl.when(inner)
    def _():
        for piece in pieces:
            to_cross(0, piece).start()

    for piece in pieces:
        to_mate(0, piece).start()
    for piece in pieces:
        across(2, piece).start()
    for load in loads[1:]:
        load.wait()

    def tables(position):
        shifts, live = slot_of(places[position], src_ref, off_ref, cnt_ref)
        write_tables(position, shifts, live.astype(F32), member, wz_ref, wy_ref, lx_ref)

    def products(position, waiting, total, first):
        rows = len(STEPS) // PARTS[position]
        for part in range(PARTS[position]):
            for step in STEPS[part * rows : part * rows + rows]:
                for piece in pieces if step in waiting else ():
                    arrived(position, step, piece)
            zy_products(position, part, gbuf, wz_ref, wy_ref, rbuf)
        x_products(position, total, lx_ref, rbuf, acc, first)

    note = pltpu.make_async_remote_copy(
        src_ref=info.at[0], dst_ref=info.at[1], send_sem=nsend.at[0], recv_sem=nrecv.at[0],
        device_id=(cross, member), device_id_type=MESH_ID,
    )

    @pl.when(inner)
    def _():
        shifts, live = slot_of(cross, src_ref, off_ref, cnt_ref)
        row = iota((8, TILE), 0)
        info[0] = jnp.where(
            row == 0, shifts[0], jnp.where(row == 1, shifts[1], jnp.where(row == 2, shifts[2], live))
        )
        note.start()

    tables(OWN)
    for piece in pieces:
        for step in (1, 3):
            arrived(0, step, piece)

            @pl.when(inner)
            def _():
                to_cross(step, piece).start()

            to_mate(step, piece).start()

    @pl.when(inner)
    def _():
        for piece in pieces:
            arrived(2, 0, piece)
            opposite(piece).start()

    zy_products(OWN, 0, gbuf, wz_ref, wy_ref, rbuf)
    for piece in pieces:
        arrived(0, 2, piece)
        to_mate(2, piece).start()
    tables(MATE)
    zy_products(OWN, 1, gbuf, wz_ref, wy_ref, rbuf)
    x_products(OWN, 0, lx_ref, rbuf, acc, True)
    products(MATE, STEPS, 0, False)

    def exchange(buffer, places_from, send, recv):
        return [
            pltpu.make_async_remote_copy(
                src_ref=buffer.at[source], dst_ref=buffer.at[place],
                send_sem=send.at[place - 1], recv_sem=recv.at[place - 1],
                device_id=(places[place], member), device_id_type=MESH_ID,
            )
            for place, source in zip((FAR, MATE), places_from)
        ]

    def act(copies, name):
        @pl.when(inner)
        def _():
            getattr(copies[0], name)()

        getattr(copies[1], name)()

    def pick(buffer, face, index, shape):
        source = jnp.full(shape, nb_ref[0, face], jnp.int32)
        parts = [buffer[place, index].reshape(shape) for place in range(3)]
        chosen = jnp.where(source == patch, parts[0], jnp.where(source == mate, parts[1], parts[2]))
        return jnp.where(source < 0, 0.0, chosen)

    def ghosts(buffer, rows, z_count, y_count, x_count):
        shape = (rows, 128)
        groups = rows // 8
        lane = iota(shape, 1)
        zs, ys, xs = [], [], []
        for u in range(2):
            index = pl.ds(u * groups, groups)
            zs.append(jnp.where((lane & 1) == 1, pick(buffer, 5, index, shape), pick(buffer, 4, index, shape)))
        at = 2 * groups
        for j in range(y_count):
            index = pl.ds(at, groups)
            ys.append(jnp.where(lane < 64, pick(buffer, 3, index, shape), pick(buffer, 2, index, shape)))
            at += groups
        shape = (2, 8, 128)
        row = iota(shape, 1)
        for j in range(x_count):
            index = pl.ds(at, 2)
            xs.append(jnp.where(row < 4, pick(buffer, 0, index, shape), pick(buffer, 1, index, shape)))
            at += 2
        return zs, ys, xs

    def pack_potential(fields, store):
        px, py, pz = fields
        packs = pack_z([px, py], HALO) + [pack_y(px, HALO), pack_y(pz, HALO)]
        for index, part in enumerate(packs):
            store(pl.ds(2 * index, 2), part.reshape(2, 8, 128))
        for index, part in enumerate(pack_x([py, pz], member)):
            store(pl.ds(8 + 2 * index, 2), part)

    def into(buffer, place):
        def store(index, part):
            buffer[place, index] = part

        return store

    copies = exchange(pbuf, (3, 0), psend, precv)
    near = potential_of(acc, 0)
    for i in range(COMPONENTS):
        potential[i] = near[i]

    @pl.when(inner)
    def _():
        pack_potential(near, into(pbuf, 3))
        copies[0].start()
        tables(FAR)
        note.wait_recv()
        sent = info[1]
        write_tables(
            BACK, (sent[0:1, :128], sent[1:2], sent[2:3]), sent[3:4, :128].astype(F32),
            member, wz_ref, wy_ref, lx_ref,
        )
        products(BACK, (), 1, True)
        pack_potential(potential_of(acc, 1), into(back, 0))
        products(FAR, STEPS[1:], 2, True)
        far = potential_of(acc, 2)
        for i in range(COMPONENTS):
            potential[i] = potential[i] + far[i]

    @pl.when(jnp.logical_not(inner))
    def _():
        pbuf[FAR] = jnp.zeros(pbuf.shape[1:], F32)
        vbuf[FAR] = jnp.zeros(vbuf.shape[1:], F32)

    px, py, pz = [potential[i] for i in range(COMPONENTS)]
    pack_potential((px, py, pz), into(pbuf, 0))
    copies[1].start()

    @pl.when(inner)
    def _():
        copies[0].wait_recv()
        pbuf[FAR] = pbuf[FAR] + back[0]

    copies[1].wait_recv()
    zs, ys, xs = ghosts(pbuf, HALO, 2, 2, 2)
    above, below = unpack_z(zs, 2, HALO)
    vx = grad_y(pz, ys[1], HALO) - grad_z(py, above[1], below[1])
    vy = grad_z(px, above[0], below[0]) - grad_x(pz, xs[1], member, False)
    vz = grad_x(py, xs[0], member, False) - grad_y(px, ys[0], HALO)
    velocity = [vx, vy, vz]
    own = [own_rows(v) for v in velocity]
    packs = pack_z(own, 8) + [pack_y(v, 8) for v in own]
    for index, part in enumerate(packs):
        vbuf[0, index] = part
    for index, part in enumerate(pack_x(velocity, member)):
        vbuf[0, 5 + 2 * index : 7 + 2 * index] = part
    vcopies = exchange(vbuf, (0, 0), vsend, vrecv)
    act(vcopies, "start")
    for i in range(COMPONENTS):
        for v in range(8):
            out_ref[0, i, :, 128 * v : 128 * v + 128] = own[i][8 * v : 8 * v + 8]
    act(vcopies, "wait_recv")
    zs, ys, xs = ghosts(vbuf, 8, 3, 3, 3)
    above, below = unpack_z(zs, 3, 8)
    spin = [
        jnp.concatenate([vort_ref[0, i, :, 128 * v : 128 * v + 128].astype(F32) for v in range(8)], axis=0)
        for i in range(COMPONENTS)
    ]
    for i in range(COMPONENTS):
        total = (
            spin[0] * grad_x(velocity[i], xs[i], member, True)
            + spin[1] * grad_y(own[i], ys[i], 8)
            + spin[2] * grad_z(own[i], above[i], below[i])
        )
        for v in range(8):
            out_ref[0, 3 + i, :, 128 * v : 128 * v + 128] = total[8 * v : 8 * v + 8]

    for piece in pieces:
        for step in (1, 2, 3):
            across(step, piece).wait_send()
        for step in STEPS:
            to_mate(step, piece).wait_send()

    @pl.when(inner)
    def _():
        for piece in pieces:
            for step in (0, 1, 3):
                to_cross(step, piece).wait_send()
            opposite(piece).wait_send()

    @pl.when(inner)
    def _():
        note.wait_send()

    act(copies, "wait_send")
    act(vcopies, "wait_send")


def body(patches, vorticity, pair_source, pair_offset, pair_count, neighbours):
    hbm = pl.BlockSpec(memory_space=pltpu.HBM)
    vmem = pl.BlockSpec(memory_space=pltpu.VMEM)
    out = jax.ShapeDtypeStruct((1, 2 * COMPONENTS, SLAB, CELL * CELL), F32)
    both = pl.pallas_call(
        functools.partial(kernel, patches),
        out_shape=out,
        in_specs=[hbm] * 5,
        out_specs=vmem,
        scratch_shapes=[
            pltpu.SMEM((1, NEAR), jnp.int32),
            pltpu.SMEM((1, NEAR), jnp.int32),
            pltpu.SMEM((1,), jnp.int32),
            pltpu.SMEM((1, 6), jnp.int32),
            pltpu.VMEM((1, COMPONENTS, SLAB, CELL * CELL), BF16),
            pltpu.VMEM((3, PATCH_ROWS, TILE), BF16),
            pltpu.VMEM((4 * TERMS, TILE, TILE), BF16),
            pltpu.VMEM((4 * TERMS, TILE, TILE), BF16),
            pltpu.VMEM((4, HALO, 128), BF16),
            pltpu.VMEM((12, 128, TILE), BF16),
            pltpu.VMEM((3, 12, HALO, TILE), F32),
            pltpu.VMEM((COMPONENTS, 128, 128), F32),
            pltpu.VMEM((4, 12, 8, 128), F32),
            pltpu.VMEM((1, 12, 8, 128), F32),
            pltpu.VMEM((3, 11, 8, 128), F32),
            pltpu.VMEM((2, 8, TILE), jnp.int32),
            pltpu.SemaphoreType.DMA((5,)),
            pltpu.SemaphoreType.DMA((3, PIECES)),
            pltpu.SemaphoreType.DMA((MEMBERS, PIECES)),
            pltpu.SemaphoreType.DMA((MEMBERS, PIECES)),
            pltpu.SemaphoreType.DMA((3 * MEMBERS, PIECES)),
            pltpu.SemaphoreType.DMA((2,)),
            pltpu.SemaphoreType.DMA((2,)),
            pltpu.SemaphoreType.DMA((2,)),
            pltpu.SemaphoreType.DMA((2,)),
            pltpu.SemaphoreType.DMA((1,)),
            pltpu.SemaphoreType.DMA((1,)),
        ],
        compiler_params=pltpu.CompilerParams(
            collective_id=0, has_side_effects=True, vmem_limit_bytes=40 << 20
        ),
    )(pair_source, pair_offset, pair_count, neighbours, vorticity)
    return both[:, :3], both[:, 3:]


def solution(mesh):
    return jax.shard_map(
        functools.partial(body, mesh.shape["patch"]),
        mesh=mesh,
        in_specs=(
            P("patch", None, "comp", None),
            P("patch", None),
            P("patch", None),
            P("patch"),
            P("patch", None),
        ),
        out_specs=(P("patch", None, "comp", None), P("patch", None, "comp", None)),
        check_vma=False,
    )
```

```python
import functools

import jax
import jax.numpy as jnp
from jax import lax
from jax.experimental import pallas as pl
from jax.experimental.pallas import tpu as pltpu
from jax.sharding import PartitionSpec as P

CELL = 32
TERMS = 4
NEAR = 3
MEMBERS = 4
SLAB = CELL // MEMBERS
COMPONENTS = 3
CHUNK = 4 * COMPONENTS * SLAB
PATCH_ROWS = MEMBERS * CHUNK
TILE = 256
HALO = 16
W0 = 0.08 / 0.75 ** 0.5
F32 = jnp.float32
BF16 = jnp.bfloat16
MESH_ID = pl.DeviceIdType.MESH
STEPS = (0, 1, 3, 2)
SLOT = {step: slot for slot, step in enumerate(STEPS)}
PIECES = 1
OWN, MATE, FAR, BACK = range(4)
SOURCES = (OWN, MATE, FAR, OWN)
PARTS = (2, 1, 2, 1)


def iota(shape, dim):
    return lax.broadcasted_iota(jnp.int32, shape, dim)


def lane_roll(values, shift):
    shift = shift % 128
    return values if shift == 0 else pltpu.roll(values, shift, values.ndim - 1)


def row_roll(values, shift):
    shift = shift % 8
    if shift == 0:
        return values
    grouped = values.reshape(-1, 8, 128)
    return pltpu.roll(grouped, shift, 1).reshape(values.shape)


def slot_of(source, src_ref, off_ref, cnt_ref):
    code = jnp.int32(13)
    live = jnp.int32(0)
    count = cnt_ref[0]
    for j in range(NEAR):
        hit = (count > j) & (src_ref[0, j] == source)
        code = jnp.where(hit, off_ref[0, j], code)
        live = jnp.where(hit, 1, live)
    shifts = (lax.div(code, 9) - 1, lax.rem(lax.div(code, 3), 3) - 1, lax.rem(code, 3) - 1)
    return shifts, live


def gauss(spacing, scale):
    spacing = spacing.astype(F32)
    return jnp.exp(-(spacing * spacing / 1.125) * scale)


def write_tables(position, shifts, live, member, wz_ref, wy_ref, lx_ref):
    shift_x, shift_y, shift_z = shifts
    rows = iota((CELL, TILE), 0)
    cols = iota((CELL, TILE), 1)
    gap_z = (cols >> 3) - rows - CELL * shift_z
    gap_y = ((cols >> 5) + 8 * ((cols >> 3) & 3)) - rows - CELL * shift_y
    low = cols & 7
    low8 = iota((8, TILE), 1) & 7
    for k in range(TERMS):
        scale = 1.0 / 16.0 ** k
        table = gauss(gap_z, scale)
        wz_ref[position * TERMS + k] = jnp.concatenate(
            [jnp.where(low == y, table, 0.0) for y in range(8)], axis=0
        ).astype(BF16)
        table = gauss(gap_y, scale)
        wy_ref[position * TERMS + k] = jnp.concatenate(
            [jnp.where(low8 == z, table[8 * h : 8 * h + 8], 0.0) for h in range(4) for z in range(8)],
            axis=0,
        ).astype(BF16)
    row = iota((HALO, 128), 0)
    col = iota((HALO, 128), 1)
    plane = (SLAB * member + jnp.where(row < 12, row, row - HALO)) & (CELL - 1)
    if PARTS[position] == 1:
        term = col >> 5
        slot = (col >> 3) & 3
    else:
        term = (col >> 4) & 3
        slot = 2 * (col >> 6) + ((col >> 3) & 1)
    step = slot ^ (slot >> 1)
    source = SLAB * ((member + step) & 3) + (col & 7)
    scale = jnp.where(term == 0, 1.0, jnp.where(term == 1, 1 / 16, jnp.where(term == 2, 1 / 256, 1 / 4096)))
    weight = jnp.where(term == 0, 1.0, jnp.where(term == 1, 0.5, jnp.where(term == 2, 0.25, 0.125)))
    table = gauss(plane - source - CELL * shift_x, scale).astype(BF16).astype(F32)
    lx_ref[position] = (table * weight * live).astype(BF16)


def zy_products(position, part, gbuf, wz_ref, wy_ref, sbuf, rbuf):
    slots = MEMBERS // PARTS[position]
    rows = slots * CHUNK
    lower = iota((slots, 24, 128), 2) < 64
    for k in range(TERMS):
        along_z = jnp.dot(
            gbuf[SOURCES[position], part * rows : part * rows + rows],
            wz_ref[position * TERMS + k],
            preferred_element_type=F32,
        ).reshape(slots, 4, 24, TILE)
        blocks = [[None] * 2 for _ in range(4)]
        for pair in range(2):
            for half in range(2):
                a = along_z[:, 2 * pair, :, 128 * half : 128 * half + 128]
                b = along_z[:, 2 * pair + 1, :, 128 * half : 128 * half + 128]
                blocks[2 * half][pair] = jnp.where(lower, a, lane_roll(b, 64))
                blocks[2 * half + 1][pair] = jnp.where(lower, lane_roll(a, 64), b)
        pieces = []
        for block in blocks:
            joined = jnp.concatenate(block, axis=2)
            for i in range(COMPONENTS):
                pieces.append(joined[:, 8 * i : 8 * i + 8].reshape(8 * slots, TILE))
        sbuf[k, :rows] = jnp.concatenate(pieces, axis=0).astype(BF16)
    for k in range(TERMS):
        along_y = jnp.dot(
            sbuf[k, :rows], wy_ref[position * TERMS + k], preferred_element_type=F32
        ).astype(BF16)
        at = (part * TERMS + k) * 8 * slots
        rbuf[:, at : at + 8 * slots, :] = along_y.reshape(12, 8 * slots, TILE)


def x_products(position, total, lx_ref, rbuf, acc, first):
    for block in range(12):
        term = jnp.dot(lx_ref[position], rbuf[block], preferred_element_type=F32)
        acc[total, block] = term if first else acc[total, block] + term


def potential_of(acc, total):
    lane = iota((2 * HALO, 128), 1)
    bit4 = (lane & 16) == 0
    bit3 = (lane & 8) == 0
    out = []
    for i in range(COMPONENTS):
        a = []
        for block in range(4):
            tile = acc[total, 3 * block + i] * W0
            a.append(jnp.concatenate([tile[:, :128], tile[:, 128:]], axis=0))
        b = [
            jnp.where(bit4, a[0], lane_roll(a[2], 16)),
            jnp.where(bit4, a[1], lane_roll(a[3], 16)),
            jnp.where(bit4, lane_roll(a[0], -16), a[2]),
            jnp.where(bit4, lane_roll(a[1], -16), a[3]),
        ]
        d = [
            jnp.where(bit3, b[0], lane_roll(b[1], 8)),
            jnp.where(bit3, lane_roll(b[0], -8), b[1]),
            jnp.where(bit3, b[2], lane_roll(b[3], 8)),
            jnp.where(bit3, lane_roll(b[2], -8), b[3]),
        ]
        out.append(jnp.concatenate(d, axis=0))
    return out


def z_slots(count):
    for j in range(count):
        for v in range(8):
            yield j, v, v % 2, 2 * (count * (v // 2) + j) + 1


def pack_z(fields, rows):
    shape = (rows, 128)
    lane = iota(shape, 1) & 31
    packed = [jnp.zeros(shape, F32)] * 2
    for j, v, u, s in z_slots(len(fields)):
        mine = (lane == s) | (lane == s - 1)
        packed[u] = jnp.where(mine, lane_roll(fields[j][rows * v : rows * v + rows], s), packed[u])
    return packed


def unpack_z(packed, count, rows):
    above = [[None] * 8 for _ in range(count)]
    below = [[None] * 8 for _ in range(count)]
    for j, v, u, s in z_slots(count):
        above[j][v] = lane_roll(packed[u], 31 - s)
        below[j][v] = lane_roll(packed[u], 97 - s)
    return (
        [jnp.concatenate(x, axis=0) for x in above],
        [jnp.concatenate(x, axis=0) for x in below],
    )


def grad_z(field, above, below):
    z = iota(field.shape, 1) & 31
    higher = jnp.where(z == 31, above, lane_roll(field, -1))
    lower = jnp.where(z == 0, below, lane_roll(field, 1))
    return 0.5 * (higher - lower)


def pack_y(field, rows):
    lower = iota((rows, 128), 1) < 64
    return jnp.where(lower, field[:rows], field[7 * rows :])


def grad_y(field, ghost, rows):
    lane = iota(field.shape, 1)
    moved = lane_roll(field, -32)
    following = jnp.concatenate([moved[rows:], lane_roll(ghost, -32)], axis=0)
    higher = jnp.where(lane < 96, moved, following)
    moved = lane_roll(field, 32)
    previous = jnp.concatenate([lane_roll(ghost, 32), moved[:-rows]], axis=0)
    lower = jnp.where(lane >= 32, moved, previous)
    return 0.5 * (higher - lower)


def halves(field):
    grouped = field.reshape(8, 2, 8, 128)
    return grouped[:, 0], grouped[:, 1]


def pack_x(fields, member):
    groups = []
    for field in fields:
        low, high = halves(field)
        at_end = jnp.full(low.shape, member, jnp.int32) == MEMBERS - 1
        first = jnp.where(at_end, high, low)
        last = jnp.where(at_end, low, high)
        row = iota((2, 8, 128), 1)
        packed = jnp.zeros((2, 8, 128), F32)
        for s in range(4):
            a = pltpu.roll(first[2 * s : 2 * s + 2], 7 - s, 1)
            b = pltpu.roll(last[2 * s : 2 * s + 2], s + 1, 1)
            packed = jnp.where(row == 7 - s, a, jnp.where(row == s, b, packed))
        groups.append(packed)
    return groups


def unpack_x(packed):
    above = jnp.concatenate([packed if s == 0 else pltpu.roll(packed, s, 1) for s in range(4)], axis=0)
    below = jnp.concatenate([packed if s == 0 else pltpu.roll(packed, 8 - s, 1) for s in range(4)], axis=0)
    return above, below


def grad_x(field, packed, member, own_only):
    low, high = halves(field)
    above, below = unpack_x(packed)
    row = iota(low.shape, 1)
    device = jnp.full(low.shape, member, jnp.int32)
    first = device == 0
    last = device == MEMBERS - 1
    moved_low = pltpu.roll(low, 7, 1)
    moved_high = pltpu.roll(high, 7, 1)
    up_low = jnp.where(row == 7, jnp.where(last, above, moved_high), moved_low)
    back_low = pltpu.roll(low, 1, 1)
    back_high = pltpu.roll(high, 1, 1)
    down_low = jnp.where(row == 0, jnp.where(first, below, back_high), back_low)
    own = 0.5 * (up_low - down_low)
    if own_only:
        return own.reshape(64, 128)
    up_high = jnp.where(row == 7, jnp.where(first, above, moved_low), moved_high)
    down_high = jnp.where(row == 0, jnp.where(last, below, back_low), back_high)
    other = 0.5 * (up_high - down_high)
    return jnp.stack([own, other], axis=1).reshape(128, 128)


def own_rows(field):
    return halves(field)[0].reshape(64, 128)


def kernel(patches, src_hbm, off_hbm, cnt_hbm, nb_hbm, vort_hbm, out_ref,
           src_ref, off_ref, cnt_ref, nb_ref, vort_ref,
           gbuf, wz_ref, wy_ref, lx_ref, sbuf, rbuf, acc, potential, pbuf, back, vbuf, info,
           isem, xsend, msend, csend, grecv, psend, precv, vsend, vrecv, nsend, nrecv):
    patch = lax.axis_index("patch")
    member = lax.axis_index("comp")
    odd = lax.rem(patch, 2)
    mate = patch + 1 - 2 * odd
    cross = lax.rem(patch + patches - 1 + 2 * odd, patches)
    places = (patch, mate, cross)
    inner = (patch > 0) & (patch < patches - 1)

    def chunk(position, step, piece):
        rows = CHUNK // PIECES
        return gbuf.at[position, pl.ds(SLOT[step % MEMBERS] * CHUNK + piece * rows, rows)]

    def other(step):
        return lax.rem(member + step, MEMBERS)

    barrier = pltpu.get_barrier_semaphore()

    def greet(partner):
        pl.semaphore_signal(barrier, inc=1, device_id=partner, device_id_type=MESH_ID)

    @pl.when(inner)
    def _():
        greet((cross, member))

    for step in STEPS[1:]:
        greet((patch, other(step)))
    greet((mate, member))

    inputs = ((vort_hbm, vort_ref), (src_hbm, src_ref), (off_hbm, off_ref), (cnt_hbm, cnt_ref), (nb_hbm, nb_ref))
    loads = [pltpu.make_async_copy(a, b, isem.at[n]) for n, (a, b) in enumerate(inputs)]
    for load in loads:
        load.start()
    loads[0].wait()
    cells = [vort_ref[0, i].astype(F32) for i in range(COMPONENTS)]
    staged = jnp.concatenate(
        [cells[i][:, TILE * q : TILE * q + TILE] for q in range(4) for i in range(COMPONENTS)], axis=0
    ).astype(BF16)
    gbuf[0, :CHUNK, :] = staged
    pl.semaphore_wait(barrier, jnp.where(inner, 5, 4))

    def send(position, step, piece, target, place, landing, send_sem):
        return pltpu.make_async_remote_copy(
            src_ref=chunk(position, step, piece), dst_ref=chunk(place, landing, piece),
            send_sem=send_sem, recv_sem=grecv.at[place * MEMBERS + SLOT[landing % MEMBERS], piece],
            device_id=target, device_id_type=MESH_ID,
        )

    def across(step, piece):
        return send(0, 0, piece, (patch, other(step)), 0, -step, xsend.at[step - 1, piece])

    def to_mate(step, piece):
        return send(0, step, piece, (mate, member), 1, step, msend.at[step, piece])

    def to_cross(step, piece):
        return send(0, step, piece, (cross, member), 2, step, csend.at[step, piece])

    def opposite(piece):
        return send(2, 0, piece, (patch, other(2)), 2, 2, csend.at[2, piece])

    def arrived(position, step, piece):
        pltpu.make_async_remote_copy(
            src_ref=chunk(position, step, piece), dst_ref=chunk(position, step, piece),
            send_sem=xsend.at[0, 0], recv_sem=grecv.at[position * MEMBERS + SLOT[step], piece],
            device_id=(cross, member), device_id_type=MESH_ID,
        ).wait_recv()

    pieces = range(PIECES)
    for step in (1, 3):
        for piece in pieces:
            across(step, piece).start()

    @pl.when(inner)
    def _():
        for piece in pieces:
            to_cross(0, piece).start()

    for piece in pieces:
        to_mate(0, piece).start()
    for piece in pieces:
        across(2, piece).start()
    for load in loads[1:]:
        load.wait()

    def tables(position):
        shifts, live = slot_of(places[position], src_ref, off_ref, cnt_ref)
        write_tables(position, shifts, live.astype(F32), member, wz_ref, wy_ref, lx_ref)

    def products(position, waiting, total, first):
        rows = len(STEPS) // PARTS[position]
        for part in range(PARTS[position]):
            for step in STEPS[part * rows : part * rows + rows]:
                for piece in pieces if step in waiting else ():
                    arrived(position, step, piece)
            zy_products(position, part, gbuf, wz_ref, wy_ref, sbuf, rbuf)
        x_products(position, total, lx_ref, rbuf, acc, first)

    note = pltpu.make_async_remote_copy(
        src_ref=info.at[0], dst_ref=info.at[1], send_sem=nsend.at[0], recv_sem=nrecv.at[0],
        device_id=(cross, member), device_id_type=MESH_ID,
    )

    @pl.when(inner)
    def _():
        shifts, live = slot_of(cross, src_ref, off_ref, cnt_ref)
        row = iota((8, TILE), 0)
        info[0] = jnp.where(
            row == 0, shifts[0], jnp.where(row == 1, shifts[1], jnp.where(row == 2, shifts[2], live))
        )
        note.start()

    for position in (OWN, MATE, FAR):
        tables(position)
    for piece in pieces:
        for step in (1, 3):
            arrived(0, step, piece)

            @pl.when(inner)
            def _():
                to_cross(step, piece).start()

            to_mate(step, piece).start()

    @pl.when(inner)
    def _():
        for piece in pieces:
            arrived(2, 0, piece)
            opposite(piece).start()

    zy_products(OWN, 0, gbuf, wz_ref, wy_ref, sbuf, rbuf)
    for piece in pieces:
        arrived(0, 2, piece)
        to_mate(2, piece).start()
    zy_products(OWN, 1, gbuf, wz_ref, wy_ref, sbuf, rbuf)
    x_products(OWN, 0, lx_ref, rbuf, acc, True)
    products(MATE, STEPS, 0, False)

    def exchange(buffer, places_from, send, recv):
        return [
            pltpu.make_async_remote_copy(
                src_ref=buffer.at[source], dst_ref=buffer.at[place],
                send_sem=send.at[place - 1], recv_sem=recv.at[place - 1],
                device_id=(places[place], member), device_id_type=MESH_ID,
            )
            for place, source in zip((FAR, MATE), places_from)
        ]

    def act(copies, name):
        @pl.when(inner)
        def _():
            getattr(copies[0], name)()

        getattr(copies[1], name)()

    def pick(buffer, face, index, shape):
        source = jnp.full(shape, nb_ref[0, face], jnp.int32)
        parts = [buffer[place, index].reshape(shape) for place in range(3)]
        chosen = jnp.where(source == patch, parts[0], jnp.where(source == mate, parts[1], parts[2]))
        return jnp.where(source < 0, 0.0, chosen)

    def ghosts(buffer, rows, z_count, y_count, x_count):
        shape = (rows, 128)
        groups = rows // 8
        lane = iota(shape, 1)
        zs, ys, xs = [], [], []
        for u in range(2):
            index = pl.ds(u * groups, groups)
            zs.append(jnp.where((lane & 1) == 1, pick(buffer, 5, index, shape), pick(buffer, 4, index, shape)))
        at = 2 * groups
        for j in range(y_count):
            index = pl.ds(at, groups)
            ys.append(jnp.where(lane < 64, pick(buffer, 3, index, shape), pick(buffer, 2, index, shape)))
            at += groups
        shape = (2, 8, 128)
        row = iota(shape, 1)
        for j in range(x_count):
            index = pl.ds(at, 2)
            xs.append(jnp.where(row < 4, pick(buffer, 0, index, shape), pick(buffer, 1, index, shape)))
            at += 2
        return zs, ys, xs

    def pack_potential(fields, store):
        px, py, pz = fields
        packs = pack_z([px, py], HALO) + [pack_y(px, HALO), pack_y(pz, HALO)]
        for index, part in enumerate(packs):
            store(pl.ds(2 * index, 2), part.reshape(2, 8, 128))
        for index, part in enumerate(pack_x([py, pz], member)):
            store(pl.ds(8 + 2 * index, 2), part)

    def into(buffer, place):
        def store(index, part):
            buffer[place, index] = part

        return store

    copies = exchange(pbuf, (3, 0), psend, precv)
    near = potential_of(acc, 0)
    for i in range(COMPONENTS):
        potential[i] = near[i]

    @pl.when(inner)
    def _():
        pack_potential(near, into(pbuf, 3))
        copies[0].start()
        products(FAR, STEPS[1:], 2, True)
        far = potential_of(acc, 2)
        for i in range(COMPONENTS):
            potential[i] = potential[i] + far[i]

    @pl.when(jnp.logical_not(inner))
    def _():
        pbuf[FAR] = jnp.zeros(pbuf.shape[1:], F32)
        vbuf[FAR] = jnp.zeros(vbuf.shape[1:], F32)

    px, py, pz = [potential[i] for i in range(COMPONENTS)]
    pack_potential((px, py, pz), into(pbuf, 0))
    copies[1].start()

    @pl.when(inner)
    def _():
        note.wait_recv()
        sent = info[1]
        write_tables(
            BACK, (sent[0:1, :128], sent[1:2], sent[2:3]), sent[3:4, :128].astype(F32),
            member, wz_ref, wy_ref, lx_ref,
        )
        products(BACK, (), 1, True)
        pack_potential(potential_of(acc, 1), into(back, 0))
        copies[0].wait_recv()
        pbuf[FAR] = pbuf[FAR] + back[0]

    copies[1].wait_recv()
    zs, ys, xs = ghosts(pbuf, HALO, 2, 2, 2)
    above, below = unpack_z(zs, 2, HALO)
    vx = grad_y(pz, ys[1], HALO) - grad_z(py, above[1], below[1])
    vy = grad_z(px, above[0], below[0]) - grad_x(pz, xs[1], member, False)
    vz = grad_x(py, xs[0], member, False) - grad_y(px, ys[0], HALO)
    velocity = [vx, vy, vz]
    own = [own_rows(v) for v in velocity]
    packs = pack_z(own, 8) + [pack_y(v, 8) for v in own]
    for index, part in enumerate(packs):
        vbuf[0, index] = part
    for index, part in enumerate(pack_x(velocity, member)):
        vbuf[0, 5 + 2 * index : 7 + 2 * index] = part
    vcopies = exchange(vbuf, (0, 0), vsend, vrecv)
    act(vcopies, "start")
    for i in range(COMPONENTS):
        for v in range(8):
            out_ref[0, i, :, 128 * v : 128 * v + 128] = own[i][8 * v : 8 * v + 8]
    act(vcopies, "wait_recv")
    zs, ys, xs = ghosts(vbuf, 8, 3, 3, 3)
    above, below = unpack_z(zs, 3, 8)
    spin = [
        jnp.concatenate([vort_ref[0, i, :, 128 * v : 128 * v + 128].astype(F32) for v in range(8)], axis=0)
        for i in range(COMPONENTS)
    ]
    for i in range(COMPONENTS):
        total = (
            spin[0] * grad_x(velocity[i], xs[i], member, True)
            + spin[1] * grad_y(own[i], ys[i], 8)
            + spin[2] * grad_z(own[i], above[i], below[i])
        )
        for v in range(8):
            out_ref[0, 3 + i, :, 128 * v : 128 * v + 128] = total[8 * v : 8 * v + 8]

    for piece in pieces:
        for step in (1, 2, 3):
            across(step, piece).wait_send()
        for step in STEPS:
            to_mate(step, piece).wait_send()

    @pl.when(inner)
    def _():
        for piece in pieces:
            for step in (0, 1, 3):
                to_cross(step, piece).wait_send()
            opposite(piece).wait_send()

    @pl.when(inner)
    def _():
        note.wait_send()

    act(copies, "wait_send")
    act(vcopies, "wait_send")


def body(patches, vorticity, pair_source, pair_offset, pair_count, neighbours):
    hbm = pl.BlockSpec(memory_space=pltpu.HBM)
    vmem = pl.BlockSpec(memory_space=pltpu.VMEM)
    out = jax.ShapeDtypeStruct((1, 2 * COMPONENTS, SLAB, CELL * CELL), F32)
    both = pl.pallas_call(
        functools.partial(kernel, patches),
        out_shape=out,
        in_specs=[hbm] * 5,
        out_specs=vmem,
        scratch_shapes=[
            pltpu.SMEM((1, NEAR), jnp.int32),
            pltpu.SMEM((1, NEAR), jnp.int32),
            pltpu.SMEM((1,), jnp.int32),
            pltpu.SMEM((1, 6), jnp.int32),
            pltpu.VMEM((1, COMPONENTS, SLAB, CELL * CELL), BF16),
            pltpu.VMEM((3, PATCH_ROWS, TILE), BF16),
            pltpu.VMEM((4 * TERMS, TILE, TILE), BF16),
            pltpu.VMEM((4 * TERMS, TILE, TILE), BF16),
            pltpu.VMEM((4, HALO, 128), BF16),
            pltpu.VMEM((TERMS, PATCH_ROWS, TILE), BF16),
            pltpu.VMEM((12, 128, TILE), BF16),
            pltpu.VMEM((3, 12, HALO, TILE), F32),
            pltpu.VMEM((COMPONENTS, 128, 128), F32),
            pltpu.VMEM((4, 12, 8, 128), F32),
            pltpu.VMEM((1, 12, 8, 128), F32),
            pltpu.VMEM((3, 11, 8, 128), F32),
            pltpu.VMEM((2, 8, TILE), jnp.int32),
            pltpu.SemaphoreType.DMA((5,)),
            pltpu.SemaphoreType.DMA((3, PIECES)),
            pltpu.SemaphoreType.DMA((MEMBERS, PIECES)),
            pltpu.SemaphoreType.DMA((MEMBERS, PIECES)),
            pltpu.SemaphoreType.DMA((3 * MEMBERS, PIECES)),
            pltpu.SemaphoreType.DMA((2,)),
            pltpu.SemaphoreType.DMA((2,)),
            pltpu.SemaphoreType.DMA((2,)),
            pltpu.SemaphoreType.DMA((2,)),
            pltpu.SemaphoreType.DMA((1,)),
            pltpu.SemaphoreType.DMA((1,)),
        ],
        compiler_params=pltpu.CompilerParams(
            collective_id=0, has_side_effects=True, vmem_limit_bytes=40 << 20
        ),
    )(pair_source, pair_offset, pair_count, neighbours, vorticity)
    return both[:, :3], both[:, 3:]


def solution(mesh):
    return jax.shard_map(
        functools.partial(body, mesh.shape["patch"]),
        mesh=mesh,
        in_specs=(
            P("patch", None, "comp", None),
            P("patch", None),
            P("patch", None),
            P("patch"),
            P("patch", None),
        ),
        out_specs=(P("patch", None, "comp", None), P("patch", None, "comp", None)),
        check_vma=False,
    )
```

```python
import functools

import jax
import jax.numpy as jnp
from jax import lax
from jax.experimental import pallas as pl
from jax.experimental.pallas import tpu as pltpu
from jax.sharding import PartitionSpec as P

CELL = 32
TERMS = 4
NEAR = 3
MEMBERS = 4
SLAB = CELL // MEMBERS
COMPONENTS = 3
CHUNK = 4 * COMPONENTS * SLAB
PATCH_ROWS = MEMBERS * CHUNK
TILE = 256
HALO = 16
W0 = 0.08 / 0.75 ** 0.5
F32 = jnp.float32
BF16 = jnp.bfloat16
MESH_ID = pl.DeviceIdType.MESH
STEPS = (0, 1, 3, 2)
SLOT = {step: slot for slot, step in enumerate(STEPS)}
PIECES = 1
OWN, MATE, FAR, BACK = range(4)
SOURCES = (OWN, MATE, FAR, OWN)
PARTS = (2, 1, 2, 1)


def iota(shape, dim):
    return lax.broadcasted_iota(jnp.int32, shape, dim)


def lane_roll(values, shift):
    shift = shift % 128
    return values if shift == 0 else pltpu.roll(values, shift, values.ndim - 1)


def row_roll(values, shift):
    shift = shift % 8
    if shift == 0:
        return values
    grouped = values.reshape(-1, 8, 128)
    return pltpu.roll(grouped, shift, 1).reshape(values.shape)


def slot_of(source, src_ref, off_ref, cnt_ref):
    code = jnp.int32(13)
    live = jnp.int32(0)
    count = cnt_ref[0]
    for j in range(NEAR):
        hit = (count > j) & (src_ref[0, j] == source)
        code = jnp.where(hit, off_ref[0, j], code)
        live = jnp.where(hit, 1, live)
    shifts = (lax.div(code, 9) - 1, lax.rem(lax.div(code, 3), 3) - 1, lax.rem(code, 3) - 1)
    return shifts, live


def gauss(spacing, scale):
    spacing = spacing.astype(F32)
    return jnp.exp(-(spacing * spacing / 1.125) * scale)


def write_tables(position, shifts, live, member, wz_ref, wy_ref, lx_ref):
    shift_x, shift_y, shift_z = shifts
    rows = iota((CELL, TILE), 0)
    cols = iota((CELL, TILE), 1)
    gap_z = (cols >> 3) - rows - CELL * shift_z
    gap_y = ((cols >> 5) + 8 * ((cols >> 3) & 3)) - rows - CELL * shift_y
    low = cols & 7
    low8 = iota((8, TILE), 1) & 7
    for k in range(TERMS):
        scale = 1.0 / 16.0 ** k
        table = gauss(gap_z, scale)
        wz_ref[position * TERMS + k] = jnp.concatenate(
            [jnp.where(low == y, table, 0.0) for y in range(8)], axis=0
        ).astype(BF16)
        table = gauss(gap_y, scale)
        wy_ref[position * TERMS + k] = jnp.concatenate(
            [jnp.where(low8 == z, table[8 * h : 8 * h + 8], 0.0) for h in range(4) for z in range(8)],
            axis=0,
        ).astype(BF16)
    row = iota((HALO, 128), 0)
    col = iota((HALO, 128), 1)
    plane = (SLAB * member + jnp.where(row < 12, row, row - HALO)) & (CELL - 1)
    if PARTS[position] == 1:
        term = col >> 5
        slot = (col >> 3) & 3
    else:
        term = (col >> 4) & 3
        slot = 2 * (col >> 6) + ((col >> 3) & 1)
    step = slot ^ (slot >> 1)
    source = SLAB * ((member + step) & 3) + (col & 7)
    scale = jnp.where(term == 0, 1.0, jnp.where(term == 1, 1 / 16, jnp.where(term == 2, 1 / 256, 1 / 4096)))
    weight = jnp.where(term == 0, 1.0, jnp.where(term == 1, 0.5, jnp.where(term == 2, 0.25, 0.125)))
    table = gauss(plane - source - CELL * shift_x, scale).astype(BF16).astype(F32)
    lx_ref[position] = (table * weight * live).astype(BF16)


def zy_products(position, part, gbuf, wz_ref, wy_ref, sbuf, rbuf):
    slots = MEMBERS // PARTS[position]
    rows = slots * CHUNK
    lower = iota((slots, 24, 128), 2) < 64
    for k in range(TERMS):
        along_z = jnp.dot(
            gbuf[SOURCES[position], part * rows : part * rows + rows],
            wz_ref[position * TERMS + k],
            preferred_element_type=F32,
        ).reshape(slots, 4, 24, TILE)
        blocks = [[None] * 2 for _ in range(4)]
        for pair in range(2):
            for half in range(2):
                a = along_z[:, 2 * pair, :, 128 * half : 128 * half + 128]
                b = along_z[:, 2 * pair + 1, :, 128 * half : 128 * half + 128]
                blocks[2 * half][pair] = jnp.where(lower, a, lane_roll(b, 64))
                blocks[2 * half + 1][pair] = jnp.where(lower, lane_roll(a, 64), b)
        pieces = []
        for block in blocks:
            joined = jnp.concatenate(block, axis=2)
            for i in range(COMPONENTS):
                pieces.append(joined[:, 8 * i : 8 * i + 8].reshape(8 * slots, TILE))
        sbuf[k, :rows] = jnp.concatenate(pieces, axis=0).astype(BF16)
    for k in range(TERMS):
        along_y = jnp.dot(
            sbuf[k, :rows], wy_ref[position * TERMS + k], preferred_element_type=F32
        ).astype(BF16)
        at = (part * TERMS + k) * 8 * slots
        rbuf[:, at : at + 8 * slots, :] = along_y.reshape(12, 8 * slots, TILE)


def x_products(position, total, lx_ref, rbuf, acc, first):
    for block in range(12):
        term = jnp.dot(lx_ref[position], rbuf[block], preferred_element_type=F32)
        acc[total, block] = term if first else acc[total, block] + term


def potential_of(acc, total):
    lane = iota((2 * HALO, 128), 1)
    bit4 = (lane & 16) == 0
    bit3 = (lane & 8) == 0
    out = []
    for i in range(COMPONENTS):
        a = []
        for block in range(4):
            tile = acc[total, 3 * block + i] * W0
            a.append(jnp.concatenate([tile[:, :128], tile[:, 128:]], axis=0))
        b = [
            jnp.where(bit4, a[0], lane_roll(a[2], 16)),
            jnp.where(bit4, a[1], lane_roll(a[3], 16)),
            jnp.where(bit4, lane_roll(a[0], -16), a[2]),
            jnp.where(bit4, lane_roll(a[1], -16), a[3]),
        ]
        d = [
            jnp.where(bit3, b[0], lane_roll(b[1], 8)),
            jnp.where(bit3, lane_roll(b[0], -8), b[1]),
            jnp.where(bit3, b[2], lane_roll(b[3], 8)),
            jnp.where(bit3, lane_roll(b[2], -8), b[3]),
        ]
        out.append(jnp.concatenate(d, axis=0))
    return out


def z_slots(count):
    for j in range(count):
        for v in range(8):
            yield j, v, v % 2, 2 * (count * (v // 2) + j) + 1


def pack_z(fields, rows):
    shape = (rows, 128)
    lane = iota(shape, 1) & 31
    packed = [jnp.zeros(shape, F32)] * 2
    for j, v, u, s in z_slots(len(fields)):
        mine = (lane == s) | (lane == s - 1)
        packed[u] = jnp.where(mine, lane_roll(fields[j][rows * v : rows * v + rows], s), packed[u])
    return packed


def unpack_z(packed, count, rows):
    above = [[None] * 8 for _ in range(count)]
    below = [[None] * 8 for _ in range(count)]
    for j, v, u, s in z_slots(count):
        above[j][v] = lane_roll(packed[u], 31 - s)
        below[j][v] = lane_roll(packed[u], 97 - s)
    return (
        [jnp.concatenate(x, axis=0) for x in above],
        [jnp.concatenate(x, axis=0) for x in below],
    )


def grad_z(field):
    z = iota(field.shape, 1) & 31
    higher = jnp.where(z == 31, 0.0, lane_roll(field, -1))
    lower = jnp.where(z == 0, 0.0, lane_roll(field, 1))
    return 0.5 * (higher - lower)


def ghost_z(above, below):
    z = iota(above.shape, 1) & 31
    return 0.5 * (jnp.where(z == 31, above, 0.0) - jnp.where(z == 0, below, 0.0))


def pack_y(field, rows):
    lower = iota((rows, 128), 1) < 64
    return jnp.where(lower, field[:rows], field[7 * rows :])


def grad_y(field, rows):
    lane = iota(field.shape, 1)
    none = jnp.zeros((rows, 128), F32)
    moved = lane_roll(field, -32)
    higher = jnp.where(lane < 96, moved, jnp.concatenate([moved[rows:], none], axis=0))
    moved = lane_roll(field, 32)
    lower = jnp.where(lane >= 32, moved, jnp.concatenate([none, moved[:-rows]], axis=0))
    return 0.5 * (higher - lower)


def ghost_y(ghost, rows):
    lane = iota((rows, 128), 1)
    top = 0.5 * jnp.where(lane < 96, 0.0, lane_roll(ghost, -32))
    bottom = -0.5 * jnp.where(lane >= 32, 0.0, lane_roll(ghost, 32))
    return jnp.concatenate([bottom, jnp.zeros((6 * rows, 128), F32), top], axis=0)


def halves(field):
    grouped = field.reshape(8, 2, 8, 128)
    return grouped[:, 0], grouped[:, 1]


def pack_x(fields, member):
    groups = []
    for field in fields:
        low, high = halves(field)
        at_end = jnp.full(low.shape, member, jnp.int32) == MEMBERS - 1
        first = jnp.where(at_end, high, low)
        last = jnp.where(at_end, low, high)
        row = iota((2, 8, 128), 1)
        packed = jnp.zeros((2, 8, 128), F32)
        for s in range(4):
            a = pltpu.roll(first[2 * s : 2 * s + 2], 7 - s, 1)
            b = pltpu.roll(last[2 * s : 2 * s + 2], s + 1, 1)
            packed = jnp.where(row == 7 - s, a, jnp.where(row == s, b, packed))
        groups.append(packed)
    return groups


def unpack_x(packed):
    above = jnp.concatenate([packed if s == 0 else pltpu.roll(packed, s, 1) for s in range(4)], axis=0)
    below = jnp.concatenate([packed if s == 0 else pltpu.roll(packed, 8 - s, 1) for s in range(4)], axis=0)
    return above, below


def grad_x(field, member, own_only):
    low, high = halves(field)
    row = iota(low.shape, 1)
    device = jnp.full(low.shape, member, jnp.int32)
    first = device == 0
    last = device == MEMBERS - 1
    moved_low = pltpu.roll(low, 7, 1)
    moved_high = pltpu.roll(high, 7, 1)
    up_low = jnp.where(row == 7, jnp.where(last, 0.0, moved_high), moved_low)
    back_low = pltpu.roll(low, 1, 1)
    back_high = pltpu.roll(high, 1, 1)
    down_low = jnp.where(row == 0, jnp.where(first, 0.0, back_high), back_low)
    own = 0.5 * (up_low - down_low)
    if own_only:
        return own.reshape(64, 128)
    up_high = jnp.where(row == 7, jnp.where(first, 0.0, moved_low), moved_high)
    down_high = jnp.where(row == 0, jnp.where(last, 0.0, back_low), back_high)
    other = 0.5 * (up_high - down_high)
    return jnp.stack([own, other], axis=1).reshape(128, 128)


def ghost_x(packed, member, own_only):
    above, below = unpack_x(packed)
    row = iota(above.shape, 1)
    device = jnp.full(above.shape, member, jnp.int32)
    first = device == 0
    last = device == MEMBERS - 1
    above = 0.5 * jnp.where(row == 7, above, 0.0)
    below = 0.5 * jnp.where(row == 0, below, 0.0)
    own = jnp.where(last, above, 0.0) - jnp.where(first, below, 0.0)
    if own_only:
        return own.reshape(64, 128)
    other = jnp.where(first, above, 0.0) - jnp.where(last, below, 0.0)
    return jnp.stack([own, other], axis=1).reshape(128, 128)


def own_rows(field):
    return halves(field)[0].reshape(64, 128)


def kernel(patches, src_hbm, off_hbm, cnt_hbm, nb_hbm, vort_hbm, out_ref,
           src_ref, off_ref, cnt_ref, nb_ref, vort_ref,
           gbuf, wz_ref, wy_ref, lx_ref, sbuf, rbuf, acc, potential, flow, turning, pbuf, back, vbuf, info,
           isem, xsend, msend, csend, grecv, psend, precv, vsend, vrecv, nsend, nrecv):
    patch = lax.axis_index("patch")
    member = lax.axis_index("comp")
    odd = lax.rem(patch, 2)
    mate = patch + 1 - 2 * odd
    cross = lax.rem(patch + patches - 1 + 2 * odd, patches)
    places = (patch, mate, cross)
    inner = (patch > 0) & (patch < patches - 1)

    def chunk(position, step, piece):
        rows = CHUNK // PIECES
        return gbuf.at[position, pl.ds(SLOT[step % MEMBERS] * CHUNK + piece * rows, rows)]

    def other(step):
        return lax.rem(member + step, MEMBERS)

    barrier = pltpu.get_barrier_semaphore()

    def greet(partner):
        pl.semaphore_signal(barrier, inc=1, device_id=partner, device_id_type=MESH_ID)

    @pl.when(inner)
    def _():
        greet((cross, member))

    for step in STEPS[1:]:
        greet((patch, other(step)))
    greet((mate, member))

    inputs = ((vort_hbm, vort_ref), (src_hbm, src_ref), (off_hbm, off_ref), (cnt_hbm, cnt_ref), (nb_hbm, nb_ref))
    loads = [pltpu.make_async_copy(a, b, isem.at[n]) for n, (a, b) in enumerate(inputs)]
    for load in loads:
        load.start()
    loads[0].wait()
    cells = [vort_ref[0, i].astype(F32) for i in range(COMPONENTS)]
    staged = jnp.concatenate(
        [cells[i][:, TILE * q : TILE * q + TILE] for q in range(4) for i in range(COMPONENTS)], axis=0
    ).astype(BF16)
    gbuf[0, :CHUNK, :] = staged
    pl.semaphore_wait(barrier, jnp.where(inner, 5, 4))

    def send(position, step, piece, target, place, landing, send_sem):
        return pltpu.make_async_remote_copy(
            src_ref=chunk(position, step, piece), dst_ref=chunk(place, landing, piece),
            send_sem=send_sem, recv_sem=grecv.at[place * MEMBERS + SLOT[landing % MEMBERS], piece],
            device_id=target, device_id_type=MESH_ID,
        )

    def across(step, piece):
        return send(0, 0, piece, (patch, other(step)), 0, -step, xsend.at[step - 1, piece])

    def to_mate(step, piece):
        return send(0, step, piece, (mate, member), 1, step, msend.at[step, piece])

    def to_cross(step, piece):
        return send(0, step, piece, (cross, member), 2, step, csend.at[step, piece])

    def opposite(piece):
        return send(2, 0, piece, (patch, other(2)), 2, 2, csend.at[2, piece])

    def arrived(position, step, piece):
        pltpu.make_async_remote_copy(
            src_ref=chunk(position, step, piece), dst_ref=chunk(position, step, piece),
            send_sem=xsend.at[0, 0], recv_sem=grecv.at[position * MEMBERS + SLOT[step], piece],
            device_id=(cross, member), device_id_type=MESH_ID,
        ).wait_recv()

    pieces = range(PIECES)
    for step in (1, 3):
        for piece in pieces:
            across(step, piece).start()

    @pl.when(inner)
    def _():
        for piece in pieces:
            to_cross(0, piece).start()

    for piece in pieces:
        to_mate(0, piece).start()
    for piece in pieces:
        across(2, piece).start()
    for load in loads[1:]:
        load.wait()

    def tables(position):
        shifts, live = slot_of(places[position], src_ref, off_ref, cnt_ref)
        write_tables(position, shifts, live.astype(F32), member, wz_ref, wy_ref, lx_ref)

    def products(position, waiting, total, first):
        rows = len(STEPS) // PARTS[position]
        for part in range(PARTS[position]):
            for step in STEPS[part * rows : part * rows + rows]:
                for piece in pieces if step in waiting else ():
                    arrived(position, step, piece)
            zy_products(position, part, gbuf, wz_ref, wy_ref, sbuf, rbuf)
        x_products(position, total, lx_ref, rbuf, acc, first)

    note = pltpu.make_async_remote_copy(
        src_ref=info.at[0], dst_ref=info.at[1], send_sem=nsend.at[0], recv_sem=nrecv.at[0],
        device_id=(cross, member), device_id_type=MESH_ID,
    )

    @pl.when(inner)
    def _():
        shifts, live = slot_of(cross, src_ref, off_ref, cnt_ref)
        row = iota((8, TILE), 0)
        info[0] = jnp.where(
            row == 0, shifts[0], jnp.where(row == 1, shifts[1], jnp.where(row == 2, shifts[2], live))
        )
        note.start()

    for position in (OWN, MATE, FAR):
        tables(position)
    for piece in pieces:
        for step in (1, 3):
            arrived(0, step, piece)

            @pl.when(inner)
            def _():
                to_cross(step, piece).start()

            to_mate(step, piece).start()

    @pl.when(inner)
    def _():
        for piece in pieces:
            arrived(2, 0, piece)
            opposite(piece).start()

    zy_products(OWN, 0, gbuf, wz_ref, wy_ref, sbuf, rbuf)
    for piece in pieces:
        arrived(0, 2, piece)
        to_mate(2, piece).start()
    zy_products(OWN, 1, gbuf, wz_ref, wy_ref, sbuf, rbuf)
    x_products(OWN, 0, lx_ref, rbuf, acc, True)
    products(MATE, STEPS, 0, False)

    def exchange(buffer, places_from, send, recv):
        return [
            pltpu.make_async_remote_copy(
                src_ref=buffer.at[source], dst_ref=buffer.at[place],
                send_sem=send.at[place - 1], recv_sem=recv.at[place - 1],
                device_id=(places[place], member), device_id_type=MESH_ID,
            )
            for place, source in zip((FAR, MATE), places_from)
        ]

    def act(copies, name):
        @pl.when(inner)
        def _():
            getattr(copies[0], name)()

        getattr(copies[1], name)()

    def pick(buffer, face, index, shape):
        source = jnp.full(shape, nb_ref[0, face], jnp.int32)
        parts = [buffer[place, index].reshape(shape) for place in range(3)]
        chosen = jnp.where(source == patch, parts[0], jnp.where(source == mate, parts[1], parts[2]))
        return jnp.where(source < 0, 0.0, chosen)

    def ghosts(buffer, rows, z_count, y_count, x_count):
        shape = (rows, 128)
        groups = rows // 8
        lane = iota(shape, 1)
        zs, ys, xs = [], [], []
        for u in range(2):
            index = pl.ds(u * groups, groups)
            zs.append(jnp.where((lane & 1) == 1, pick(buffer, 5, index, shape), pick(buffer, 4, index, shape)))
        at = 2 * groups
        for j in range(y_count):
            index = pl.ds(at, groups)
            ys.append(jnp.where(lane < 64, pick(buffer, 3, index, shape), pick(buffer, 2, index, shape)))
            at += groups
        shape = (2, 8, 128)
        row = iota(shape, 1)
        for j in range(x_count):
            index = pl.ds(at, 2)
            xs.append(jnp.where(row < 4, pick(buffer, 0, index, shape), pick(buffer, 1, index, shape)))
            at += 2
        return zs, ys, xs

    def pack_potential(fields, store):
        px, py, pz = fields
        packs = pack_z([px, py], HALO) + [pack_y(px, HALO), pack_y(pz, HALO)]
        for index, part in enumerate(packs):
            store(pl.ds(2 * index, 2), part.reshape(2, 8, 128))
        for index, part in enumerate(pack_x([py, pz], member)):
            store(pl.ds(8 + 2 * index, 2), part)

    def into(buffer, place):
        def store(index, part):
            buffer[place, index] = part

        return store

    copies = exchange(pbuf, (3, 0), psend, precv)
    near = potential_of(acc, 0)
    for i in range(COMPONENTS):
        potential[i] = near[i]

    @pl.when(inner)
    def _():
        pack_potential(near, into(pbuf, 3))
        copies[0].start()
        products(FAR, STEPS[1:], 2, True)
        far = potential_of(acc, 2)
        for i in range(COMPONENTS):
            potential[i] = potential[i] + far[i]

    @pl.when(jnp.logical_not(inner))
    def _():
        pbuf[FAR] = jnp.zeros(pbuf.shape[1:], F32)
        vbuf[FAR] = jnp.zeros(vbuf.shape[1:], F32)

    px, py, pz = [potential[i] for i in range(COMPONENTS)]
    pack_potential((px, py, pz), into(pbuf, 0))
    copies[1].start()
    flow[0] = grad_y(pz, HALO) - grad_z(py)
    flow[1] = grad_z(px) - grad_x(pz, member, False)
    flow[2] = grad_x(py, member, False) - grad_y(px, HALO)

    @pl.when(inner)
    def _():
        note.wait_recv()
        sent = info[1]
        write_tables(
            BACK, (sent[0:1, :128], sent[1:2], sent[2:3]), sent[3:4, :128].astype(F32),
            member, wz_ref, wy_ref, lx_ref,
        )
        products(BACK, (), 1, True)
        pack_potential(potential_of(acc, 1), into(back, 0))
        copies[0].wait_recv()
        pbuf[FAR] = pbuf[FAR] + back[0]

    copies[1].wait_recv()
    zs, ys, xs = ghosts(pbuf, HALO, 2, 2, 2)
    above, below = unpack_z(zs, 2, HALO)
    velocity = [
        flow[0] + (ghost_y(ys[1], HALO) - ghost_z(above[1], below[1])),
        flow[1] + (ghost_z(above[0], below[0]) - ghost_x(xs[1], member, False)),
        flow[2] + (ghost_x(xs[0], member, False) - ghost_y(ys[0], HALO)),
    ]
    own = [own_rows(v) for v in velocity]
    packs = pack_z(own, 8) + [pack_y(v, 8) for v in own]
    for index, part in enumerate(packs):
        vbuf[0, index] = part
    for index, part in enumerate(pack_x(velocity, member)):
        vbuf[0, 5 + 2 * index : 7 + 2 * index] = part
    vcopies = exchange(vbuf, (0, 0), vsend, vrecv)
    act(vcopies, "start")
    for i in range(COMPONENTS):
        for v in range(8):
            out_ref[0, i, :, 128 * v : 128 * v + 128] = own[i][8 * v : 8 * v + 8]
    spin = [
        jnp.concatenate([vort_ref[0, i, :, 128 * v : 128 * v + 128].astype(F32) for v in range(8)], axis=0)
        for i in range(COMPONENTS)
    ]
    for i in range(COMPONENTS):
        flow[i, :64] = (
            spin[0] * grad_x(velocity[i], member, True)
            + spin[1] * grad_y(own[i], 8)
            + spin[2] * grad_z(own[i])
        )
        turning[i] = spin[i]
    act(vcopies, "wait_recv")
    zs, ys, xs = ghosts(vbuf, 8, 3, 3, 3)
    above, below = unpack_z(zs, 3, 8)
    for i in range(COMPONENTS):
        total = flow[i, :64] + (
            turning[0] * ghost_x(xs[i], member, True)
            + turning[1] * ghost_y(ys[i], 8)
            + turning[2] * ghost_z(above[i], below[i])
        )
        for v in range(8):
            out_ref[0, 3 + i, :, 128 * v : 128 * v + 128] = total[8 * v : 8 * v + 8]

    for piece in pieces:
        for step in (1, 2, 3):
            across(step, piece).wait_send()
        for step in STEPS:
            to_mate(step, piece).wait_send()

    @pl.when(inner)
    def _():
        for piece in pieces:
            for step in (0, 1, 3):
                to_cross(step, piece).wait_send()
            opposite(piece).wait_send()

    @pl.when(inner)
    def _():
        note.wait_send()

    act(copies, "wait_send")
    act(vcopies, "wait_send")


def body(patches, vorticity, pair_source, pair_offset, pair_count, neighbours):
    hbm = pl.BlockSpec(memory_space=pltpu.HBM)
    vmem = pl.BlockSpec(memory_space=pltpu.VMEM)
    out = jax.ShapeDtypeStruct((1, 2 * COMPONENTS, SLAB, CELL * CELL), F32)
    both = pl.pallas_call(
        functools.partial(kernel, patches),
        out_shape=out,
        in_specs=[hbm] * 5,
        out_specs=vmem,
        scratch_shapes=[
            pltpu.SMEM((1, NEAR), jnp.int32),
            pltpu.SMEM((1, NEAR), jnp.int32),
            pltpu.SMEM((1,), jnp.int32),
            pltpu.SMEM((1, 6), jnp.int32),
            pltpu.VMEM((1, COMPONENTS, SLAB, CELL * CELL), BF16),
            pltpu.VMEM((3, PATCH_ROWS, TILE), BF16),
            pltpu.VMEM((4 * TERMS, TILE, TILE), BF16),
            pltpu.VMEM((4 * TERMS, TILE, TILE), BF16),
            pltpu.VMEM((4, HALO, 128), BF16),
            pltpu.VMEM((TERMS, PATCH_ROWS, TILE), BF16),
            pltpu.VMEM((12, 128, TILE), BF16),
            pltpu.VMEM((3, 12, HALO, TILE), F32),
            pltpu.VMEM((COMPONENTS, 128, 128), F32),
            pltpu.VMEM((COMPONENTS, 128, 128), F32),
            pltpu.VMEM((COMPONENTS, 64, 128), F32),
            pltpu.VMEM((4, 12, 8, 128), F32),
            pltpu.VMEM((1, 12, 8, 128), F32),
            pltpu.VMEM((3, 11, 8, 128), F32),
            pltpu.VMEM((2, 8, TILE), jnp.int32),
            pltpu.SemaphoreType.DMA((5,)),
            pltpu.SemaphoreType.DMA((3, PIECES)),
            pltpu.SemaphoreType.DMA((MEMBERS, PIECES)),
            pltpu.SemaphoreType.DMA((MEMBERS, PIECES)),
            pltpu.SemaphoreType.DMA((3 * MEMBERS, PIECES)),
            pltpu.SemaphoreType.DMA((2,)),
            pltpu.SemaphoreType.DMA((2,)),
            pltpu.SemaphoreType.DMA((2,)),
            pltpu.SemaphoreType.DMA((2,)),
            pltpu.SemaphoreType.DMA((1,)),
            pltpu.SemaphoreType.DMA((1,)),
        ],
        compiler_params=pltpu.CompilerParams(
            collective_id=0, has_side_effects=True, vmem_limit_bytes=40 << 20
        ),
    )(pair_source, pair_offset, pair_count, neighbours, vorticity)
    return both[:, :3], both[:, 3:]


def solution(mesh):
    return jax.shard_map(
        functools.partial(body, mesh.shape["patch"]),
        mesh=mesh,
        in_specs=(
            P("patch", None, "comp", None),
            P("patch", None),
            P("patch", None),
            P("patch"),
            P("patch", None),
        ),
        out_specs=(P("patch", None, "comp", None), P("patch", None, "comp", None)),
        check_vma=False,
    )
```

```python
import functools

import jax
import jax.numpy as jnp
from jax import lax
from jax.experimental import pallas as pl
from jax.experimental.pallas import tpu as pltpu
from jax.sharding import PartitionSpec as P

CELL = 32
TERMS = 4
NEAR = 3
MEMBERS = 4
SLAB = CELL // MEMBERS
COMPONENTS = 3
CHUNK = 4 * COMPONENTS * SLAB
PATCH_ROWS = MEMBERS * CHUNK
TILE = 256
HALO = 16
W0 = 0.08 / 0.75 ** 0.5
F32 = jnp.float32
BF16 = jnp.bfloat16
MESH_ID = pl.DeviceIdType.MESH
STEPS = (0, 1, 3, 2)
SLOT = {step: slot for slot, step in enumerate(STEPS)}
PIECES = 1
OWN, MATE, FAR, BACK = range(4)
SOURCES = (OWN, MATE, FAR, OWN)
PARTS = (2, 2, 2, 1)


def iota(shape, dim):
    return lax.broadcasted_iota(jnp.int32, shape, dim)


def lane_roll(values, shift):
    shift = shift % 128
    return values if shift == 0 else pltpu.roll(values, shift, values.ndim - 1)


def row_roll(values, shift):
    shift = shift % 8
    if shift == 0:
        return values
    grouped = values.reshape(-1, 8, 128)
    return pltpu.roll(grouped, shift, 1).reshape(values.shape)


def slot_of(source, src_ref, off_ref, cnt_ref):
    code = jnp.int32(13)
    live = jnp.int32(0)
    count = cnt_ref[0]
    for j in range(NEAR):
        hit = (count > j) & (src_ref[0, j] == source)
        code = jnp.where(hit, off_ref[0, j], code)
        live = jnp.where(hit, 1, live)
    shifts = (lax.div(code, 9) - 1, lax.rem(lax.div(code, 3), 3) - 1, lax.rem(code, 3) - 1)
    return shifts, live


def gauss(spacing, scale):
    spacing = spacing.astype(F32)
    return jnp.exp(-(spacing * spacing / 1.125) * scale)


def write_tables(position, shifts, live, member, wz_ref, wy_ref, lx_ref):
    shift_x, shift_y, shift_z = shifts
    rows = iota((CELL, TILE), 0)
    cols = iota((CELL, TILE), 1)
    gap_z = (cols >> 3) - rows - CELL * shift_z
    gap_y = ((cols >> 5) + 8 * ((cols >> 3) & 3)) - rows - CELL * shift_y
    low = cols & 7
    low8 = iota((8, TILE), 1) & 7
    for k in range(TERMS):
        scale = 1.0 / 16.0 ** k
        table = gauss(gap_z, scale)
        wz_ref[position * TERMS + k] = jnp.concatenate(
            [jnp.where(low == y, table, 0.0) for y in range(8)], axis=0
        ).astype(BF16)
        table = gauss(gap_y, scale)
        wy_ref[position * TERMS + k] = jnp.concatenate(
            [jnp.where(low8 == z, table[8 * h : 8 * h + 8], 0.0) for h in range(4) for z in range(8)],
            axis=0,
        ).astype(BF16)
    row = iota((HALO, 128), 0)
    col = iota((HALO, 128), 1)
    plane = (SLAB * member + jnp.where(row < 12, row, row - HALO)) & (CELL - 1)
    if PARTS[position] == 1:
        term = col >> 5
        slot = (col >> 3) & 3
    else:
        term = (col >> 4) & 3
        slot = 2 * (col >> 6) + ((col >> 3) & 1)
    step = slot ^ (slot >> 1)
    source = SLAB * ((member + step) & 3) + (col & 7)
    scale = jnp.where(term == 0, 1.0, jnp.where(term == 1, 1 / 16, jnp.where(term == 2, 1 / 256, 1 / 4096)))
    weight = jnp.where(term == 0, 1.0, jnp.where(term == 1, 0.5, jnp.where(term == 2, 0.25, 0.125)))
    table = gauss(plane - source - CELL * shift_x, scale).astype(BF16).astype(F32)
    lx_ref[position] = (table * weight * live).astype(BF16)


def zy_products(position, part, gbuf, wz_ref, wy_ref, sbuf, rbuf):
    slots = MEMBERS // PARTS[position]
    rows = slots * CHUNK
    lower = iota((slots, 24, 128), 2) < 64
    for k in range(TERMS):
        along_z = jnp.dot(
            gbuf[SOURCES[position], part * rows : part * rows + rows],
            wz_ref[position * TERMS + k],
            preferred_element_type=F32,
        ).reshape(slots, 4, 24, TILE)
        blocks = [[None] * 2 for _ in range(4)]
        for pair in range(2):
            for half in range(2):
                a = along_z[:, 2 * pair, :, 128 * half : 128 * half + 128]
                b = along_z[:, 2 * pair + 1, :, 128 * half : 128 * half + 128]
                blocks[2 * half][pair] = jnp.where(lower, a, lane_roll(b, 64))
                blocks[2 * half + 1][pair] = jnp.where(lower, lane_roll(a, 64), b)
        pieces = []
        for block in blocks:
            joined = jnp.concatenate(block, axis=2)
            for i in range(COMPONENTS):
                pieces.append(joined[:, 8 * i : 8 * i + 8].reshape(8 * slots, TILE))
        sbuf[k, :rows] = jnp.concatenate(pieces, axis=0).astype(BF16)
    for k in range(TERMS):
        along_y = jnp.dot(
            sbuf[k, :rows], wy_ref[position * TERMS + k], preferred_element_type=F32
        ).astype(BF16)
        at = (part * TERMS + k) * 8 * slots
        rbuf[:, at : at + 8 * slots, :] = along_y.reshape(12, 8 * slots, TILE)


def x_products(position, total, lx_ref, rbuf, acc, first):
    for block in range(12):
        term = jnp.dot(lx_ref[position], rbuf[block], preferred_element_type=F32)
        acc[total, block] = term if first else acc[total, block] + term


def potential_of(acc, total):
    lane = iota((2 * HALO, 128), 1)
    bit4 = (lane & 16) == 0
    bit3 = (lane & 8) == 0
    out = []
    for i in range(COMPONENTS):
        a = []
        for block in range(4):
            tile = acc[total, 3 * block + i] * W0
            a.append(jnp.concatenate([tile[:, :128], tile[:, 128:]], axis=0))
        b = [
            jnp.where(bit4, a[0], lane_roll(a[2], 16)),
            jnp.where(bit4, a[1], lane_roll(a[3], 16)),
            jnp.where(bit4, lane_roll(a[0], -16), a[2]),
            jnp.where(bit4, lane_roll(a[1], -16), a[3]),
        ]
        d = [
            jnp.where(bit3, b[0], lane_roll(b[1], 8)),
            jnp.where(bit3, lane_roll(b[0], -8), b[1]),
            jnp.where(bit3, b[2], lane_roll(b[3], 8)),
            jnp.where(bit3, lane_roll(b[2], -8), b[3]),
        ]
        out.append(jnp.concatenate(d, axis=0))
    return out


def z_slots(count):
    for j in range(count):
        for v in range(8):
            yield j, v, v % 2, 2 * (count * (v // 2) + j) + 1


def pack_z(fields, rows):
    shape = (rows, 128)
    lane = iota(shape, 1) & 31
    packed = [jnp.zeros(shape, F32)] * 2
    for j, v, u, s in z_slots(len(fields)):
        mine = (lane == s) | (lane == s - 1)
        packed[u] = jnp.where(mine, lane_roll(fields[j][rows * v : rows * v + rows], s), packed[u])
    return packed


def unpack_z(packed, count, rows):
    above = [[None] * 8 for _ in range(count)]
    below = [[None] * 8 for _ in range(count)]
    for j, v, u, s in z_slots(count):
        above[j][v] = lane_roll(packed[u], 31 - s)
        below[j][v] = lane_roll(packed[u], 97 - s)
    return (
        [jnp.concatenate(x, axis=0) for x in above],
        [jnp.concatenate(x, axis=0) for x in below],
    )


def grad_z(field):
    z = iota(field.shape, 1) & 31
    higher = jnp.where(z == 31, 0.0, lane_roll(field, -1))
    lower = jnp.where(z == 0, 0.0, lane_roll(field, 1))
    return 0.5 * (higher - lower)


def ghost_z(above, below):
    z = iota(above.shape, 1) & 31
    return 0.5 * (jnp.where(z == 31, above, 0.0) - jnp.where(z == 0, below, 0.0))


def pack_y(field, rows):
    lower = iota((rows, 128), 1) < 64
    return jnp.where(lower, field[:rows], field[7 * rows :])


def grad_y(field, rows):
    lane = iota(field.shape, 1)
    none = jnp.zeros((rows, 128), F32)
    moved = lane_roll(field, -32)
    higher = jnp.where(lane < 96, moved, jnp.concatenate([moved[rows:], none], axis=0))
    moved = lane_roll(field, 32)
    lower = jnp.where(lane >= 32, moved, jnp.concatenate([none, moved[:-rows]], axis=0))
    return 0.5 * (higher - lower)


def ghost_y(ghost, rows):
    lane = iota((rows, 128), 1)
    top = 0.5 * jnp.where(lane < 96, 0.0, lane_roll(ghost, -32))
    bottom = -0.5 * jnp.where(lane >= 32, 0.0, lane_roll(ghost, 32))
    return jnp.concatenate([bottom, jnp.zeros((6 * rows, 128), F32), top], axis=0)


def halves(field):
    grouped = field.reshape(8, 2, 8, 128)
    return grouped[:, 0], grouped[:, 1]


def pack_x(fields, member):
    groups = []
    for field in fields:
        low, high = halves(field)
        at_end = jnp.full(low.shape, member, jnp.int32) == MEMBERS - 1
        first = jnp.where(at_end, high, low)
        last = jnp.where(at_end, low, high)
        row = iota((2, 8, 128), 1)
        packed = jnp.zeros((2, 8, 128), F32)
        for s in range(4):
            a = pltpu.roll(first[2 * s : 2 * s + 2], 7 - s, 1)
            b = pltpu.roll(last[2 * s : 2 * s + 2], s + 1, 1)
            packed = jnp.where(row == 7 - s, a, jnp.where(row == s, b, packed))
        groups.append(packed)
    return groups


def unpack_x(packed):
    above = jnp.concatenate([packed if s == 0 else pltpu.roll(packed, s, 1) for s in range(4)], axis=0)
    below = jnp.concatenate([packed if s == 0 else pltpu.roll(packed, 8 - s, 1) for s in range(4)], axis=0)
    return above, below


def grad_x(field, member, own_only):
    low, high = halves(field)
    row = iota(low.shape, 1)
    device = jnp.full(low.shape, member, jnp.int32)
    first = device == 0
    last = device == MEMBERS - 1
    moved_low = pltpu.roll(low, 7, 1)
    moved_high = pltpu.roll(high, 7, 1)
    up_low = jnp.where(row == 7, jnp.where(last, 0.0, moved_high), moved_low)
    back_low = pltpu.roll(low, 1, 1)
    back_high = pltpu.roll(high, 1, 1)
    down_low = jnp.where(row == 0, jnp.where(first, 0.0, back_high), back_low)
    own = 0.5 * (up_low - down_low)
    if own_only:
        return own.reshape(64, 128)
    up_high = jnp.where(row == 7, jnp.where(first, 0.0, moved_low), moved_high)
    down_high = jnp.where(row == 0, jnp.where(last, 0.0, back_low), back_high)
    other = 0.5 * (up_high - down_high)
    return jnp.stack([own, other], axis=1).reshape(128, 128)


def ghost_x(packed, member, own_only):
    above, below = unpack_x(packed)
    row = iota(above.shape, 1)
    device = jnp.full(above.shape, member, jnp.int32)
    first = device == 0
    last = device == MEMBERS - 1
    above = 0.5 * jnp.where(row == 7, above, 0.0)
    below = 0.5 * jnp.where(row == 0, below, 0.0)
    own = jnp.where(last, above, 0.0) - jnp.where(first, below, 0.0)
    if own_only:
        return own.reshape(64, 128)
    other = jnp.where(first, above, 0.0) - jnp.where(last, below, 0.0)
    return jnp.stack([own, other], axis=1).reshape(128, 128)


def own_rows(field):
    return halves(field)[0].reshape(64, 128)


def kernel(patches, src_hbm, off_hbm, cnt_hbm, nb_hbm, vort_hbm, out_ref,
           src_ref, off_ref, cnt_ref, nb_ref, vort_ref,
           gbuf, wz_ref, wy_ref, lx_ref, sbuf, rbuf, acc, potential, flow, turning, pbuf, back, vbuf, info,
           isem, xsend, msend, csend, grecv, psend, precv, vsend, vrecv, nsend, nrecv):
    patch = lax.axis_index("patch")
    member = lax.axis_index("comp")
    odd = lax.rem(patch, 2)
    mate = patch + 1 - 2 * odd
    cross = lax.rem(patch + patches - 1 + 2 * odd, patches)
    places = (patch, mate, cross)
    inner = (patch > 0) & (patch < patches - 1)

    def chunk(position, step, piece):
        rows = CHUNK // PIECES
        return gbuf.at[position, pl.ds(SLOT[step % MEMBERS] * CHUNK + piece * rows, rows)]

    def other(step):
        return lax.rem(member + step, MEMBERS)

    barrier = pltpu.get_barrier_semaphore()

    def greet(partner):
        pl.semaphore_signal(barrier, inc=1, device_id=partner, device_id_type=MESH_ID)

    @pl.when(inner)
    def _():
        greet((cross, member))

    for step in STEPS[1:]:
        greet((patch, other(step)))
    greet((mate, member))

    inputs = ((vort_hbm, vort_ref), (src_hbm, src_ref), (off_hbm, off_ref), (cnt_hbm, cnt_ref), (nb_hbm, nb_ref))
    loads = [pltpu.make_async_copy(a, b, isem.at[n]) for n, (a, b) in enumerate(inputs)]
    for load in loads:
        load.start()
    loads[0].wait()
    cells = [vort_ref[0, i].astype(F32) for i in range(COMPONENTS)]
    staged = jnp.concatenate(
        [cells[i][:, TILE * q : TILE * q + TILE] for q in range(4) for i in range(COMPONENTS)], axis=0
    ).astype(BF16)
    gbuf[0, :CHUNK, :] = staged
    pl.semaphore_wait(barrier, jnp.where(inner, 5, 4))

    def send(position, step, piece, target, place, landing, send_sem):
        return pltpu.make_async_remote_copy(
            src_ref=chunk(position, step, piece), dst_ref=chunk(place, landing, piece),
            send_sem=send_sem, recv_sem=grecv.at[place * MEMBERS + SLOT[landing % MEMBERS], piece],
            device_id=target, device_id_type=MESH_ID,
        )

    def across(step, piece):
        return send(0, 0, piece, (patch, other(step)), 0, -step, xsend.at[step - 1, piece])

    def to_mate(step, piece):
        return send(0, step, piece, (mate, member), 1, step, msend.at[step, piece])

    def to_cross(step, piece):
        return send(0, step, piece, (cross, member), 2, step, csend.at[step, piece])

    def opposite(piece):
        return send(2, 0, piece, (patch, other(2)), 2, 2, csend.at[2, piece])

    def arrived(position, step, piece):
        pltpu.make_async_remote_copy(
            src_ref=chunk(position, step, piece), dst_ref=chunk(position, step, piece),
            send_sem=xsend.at[0, 0], recv_sem=grecv.at[position * MEMBERS + SLOT[step], piece],
            device_id=(cross, member), device_id_type=MESH_ID,
        ).wait_recv()

    pieces = range(PIECES)
    for step in (1, 3):
        for piece in pieces:
            across(step, piece).start()

    @pl.when(inner)
    def _():
        for piece in pieces:
            to_cross(0, piece).start()

    for piece in pieces:
        to_mate(0, piece).start()
    for piece in pieces:
        across(2, piece).start()
    for load in loads[1:]:
        load.wait()

    def tables(position):
        shifts, live = slot_of(places[position], src_ref, off_ref, cnt_ref)
        write_tables(position, shifts, live.astype(F32), member, wz_ref, wy_ref, lx_ref)

    def products(position, waiting, total, first):
        rows = len(STEPS) // PARTS[position]
        for part in range(PARTS[position]):
            for step in STEPS[part * rows : part * rows + rows]:
                for piece in pieces if step in waiting else ():
                    arrived(position, step, piece)
            zy_products(position, part, gbuf, wz_ref, wy_ref, sbuf, rbuf.at[OWN])
        x_products(position, total, lx_ref, rbuf.at[OWN], acc, first)

    note = pltpu.make_async_remote_copy(
        src_ref=info.at[0], dst_ref=info.at[1], send_sem=nsend.at[0], recv_sem=nrecv.at[0],
        device_id=(cross, member), device_id_type=MESH_ID,
    )

    @pl.when(inner)
    def _():
        shifts, live = slot_of(cross, src_ref, off_ref, cnt_ref)
        row = iota((8, TILE), 0)
        info[0] = jnp.where(
            row == 0, shifts[0], jnp.where(row == 1, shifts[1], jnp.where(row == 2, shifts[2], live))
        )
        note.start()

    for position in (OWN, MATE, FAR):
        tables(position)
    for piece in pieces:
        for step in (1, 3):
            arrived(0, step, piece)

            @pl.when(inner)
            def _():
                to_cross(step, piece).start()

            to_mate(step, piece).start()

    @pl.when(inner)
    def _():
        for piece in pieces:
            arrived(2, 0, piece)
            opposite(piece).start()

    zy_products(OWN, 0, gbuf, wz_ref, wy_ref, sbuf, rbuf.at[OWN])
    for step in (0, 1):
        for piece in pieces:
            arrived(MATE, step, piece)
    zy_products(MATE, 0, gbuf, wz_ref, wy_ref, sbuf, rbuf.at[MATE])
    for piece in pieces:
        arrived(OWN, 2, piece)
        to_mate(2, piece).start()
    zy_products(OWN, 1, gbuf, wz_ref, wy_ref, sbuf, rbuf.at[OWN])
    x_products(OWN, 0, lx_ref, rbuf.at[OWN], acc, True)
    for step in (3, 2):
        for piece in pieces:
            arrived(MATE, step, piece)
    zy_products(MATE, 1, gbuf, wz_ref, wy_ref, sbuf, rbuf.at[MATE])
    x_products(MATE, 0, lx_ref, rbuf.at[MATE], acc, False)

    def exchange(buffer, places_from, send, recv):
        return [
            pltpu.make_async_remote_copy(
                src_ref=buffer.at[source], dst_ref=buffer.at[place],
                send_sem=send.at[place - 1], recv_sem=recv.at[place - 1],
                device_id=(places[place], member), device_id_type=MESH_ID,
            )
            for place, source in zip((FAR, MATE), places_from)
        ]

    def act(copies, name):
        @pl.when(inner)
        def _():
            getattr(copies[0], name)()

        getattr(copies[1], name)()

    def pick(buffer, face, index, shape):
        source = jnp.full(shape, nb_ref[0, face], jnp.int32)
        parts = [buffer[place, index].reshape(shape) for place in range(3)]
        chosen = jnp.where(source == patch, parts[0], jnp.where(source == mate, parts[1], parts[2]))
        return jnp.where(source < 0, 0.0, chosen)

    def ghosts(buffer, rows, z_count, y_count, x_count):
        shape = (rows, 128)
        groups = rows // 8
        lane = iota(shape, 1)
        zs, ys, xs = [], [], []
        for u in range(2):
            index = pl.ds(u * groups, groups)
            zs.append(jnp.where((lane & 1) == 1, pick(buffer, 5, index, shape), pick(buffer, 4, index, shape)))
        at = 2 * groups
        for j in range(y_count):
            index = pl.ds(at, groups)
            ys.append(jnp.where(lane < 64, pick(buffer, 3, index, shape), pick(buffer, 2, index, shape)))
            at += groups
        shape = (2, 8, 128)
        row = iota(shape, 1)
        for j in range(x_count):
            index = pl.ds(at, 2)
            xs.append(jnp.where(row < 4, pick(buffer, 0, index, shape), pick(buffer, 1, index, shape)))
            at += 2
        return zs, ys, xs

    def pack_potential(fields, store):
        px, py, pz = fields
        packs = pack_z([px, py], HALO) + [pack_y(px, HALO), pack_y(pz, HALO)]
        for index, part in enumerate(packs):
            store(pl.ds(2 * index, 2), part.reshape(2, 8, 128))
        for index, part in enumerate(pack_x([py, pz], member)):
            store(pl.ds(8 + 2 * index, 2), part)

    def into(buffer, place):
        def store(index, part):
            buffer[place, index] = part

        return store

    copies = exchange(pbuf, (3, 0), psend, precv)
    near = potential_of(acc, 0)
    for i in range(COMPONENTS):
        potential[i] = near[i]

    @pl.when(inner)
    def _():
        pack_potential(near, into(pbuf, 3))
        copies[0].start()
        products(FAR, STEPS[1:], 2, True)
        far = potential_of(acc, 2)
        for i in range(COMPONENTS):
            potential[i] = potential[i] + far[i]

    @pl.when(jnp.logical_not(inner))
    def _():
        pbuf[FAR] = jnp.zeros(pbuf.shape[1:], F32)
        vbuf[FAR] = jnp.zeros(vbuf.shape[1:], F32)

    px, py, pz = [potential[i] for i in range(COMPONENTS)]
    pack_potential((px, py, pz), into(pbuf, 0))
    copies[1].start()
    flow[0] = grad_y(pz, HALO) - grad_z(py)
    flow[1] = grad_z(px) - grad_x(pz, member, False)
    flow[2] = grad_x(py, member, False) - grad_y(px, HALO)

    @pl.when(inner)
    def _():
        note.wait_recv()
        sent = info[1]
        write_tables(
            BACK, (sent[0:1, :128], sent[1:2], sent[2:3]), sent[3:4, :128].astype(F32),
            member, wz_ref, wy_ref, lx_ref,
        )
        products(BACK, (), 1, True)
        pack_potential(potential_of(acc, 1), into(back, 0))
        copies[0].wait_recv()
        pbuf[FAR] = pbuf[FAR] + back[0]

    copies[1].wait_recv()
    zs, ys, xs = ghosts(pbuf, HALO, 2, 2, 2)
    above, below = unpack_z(zs, 2, HALO)
    velocity = [
        flow[0] + (ghost_y(ys[1], HALO) - ghost_z(above[1], below[1])),
        flow[1] + (ghost_z(above[0], below[0]) - ghost_x(xs[1], member, False)),
        flow[2] + (ghost_x(xs[0], member, False) - ghost_y(ys[0], HALO)),
    ]
    own = [own_rows(v) for v in velocity]
    packs = pack_z(own, 8) + [pack_y(v, 8) for v in own]
    for index, part in enumerate(packs):
        vbuf[0, index] = part
    for index, part in enumerate(pack_x(velocity, member)):
        vbuf[0, 5 + 2 * index : 7 + 2 * index] = part
    vcopies = exchange(vbuf, (0, 0), vsend, vrecv)
    act(vcopies, "start")
    for i in range(COMPONENTS):
        for v in range(8):
            out_ref[0, i, :, 128 * v : 128 * v + 128] = own[i][8 * v : 8 * v + 8]
    spin = [
        jnp.concatenate([vort_ref[0, i, :, 128 * v : 128 * v + 128].astype(F32) for v in range(8)], axis=0)
        for i in range(COMPONENTS)
    ]
    for i in range(COMPONENTS):
        flow[i, :64] = (
            spin[0] * grad_x(velocity[i], member, True)
            + spin[1] * grad_y(own[i], 8)
            + spin[2] * grad_z(own[i])
        )
        turning[i] = spin[i]
    act(vcopies, "wait_recv")
    zs, ys, xs = ghosts(vbuf, 8, 3, 3, 3)
    above, below = unpack_z(zs, 3, 8)
    for i in range(COMPONENTS):
        total = flow[i, :64] + (
            turning[0] * ghost_x(xs[i], member, True)
            + turning[1] * ghost_y(ys[i], 8)
            + turning[2] * ghost_z(above[i], below[i])
        )
        for v in range(8):
            out_ref[0, 3 + i, :, 128 * v : 128 * v + 128] = total[8 * v : 8 * v + 8]

    for piece in pieces:
        for step in (1, 2, 3):
            across(step, piece).wait_send()
        for step in STEPS:
            to_mate(step, piece).wait_send()

    @pl.when(inner)
    def _():
        for piece in pieces:
            for step in (0, 1, 3):
                to_cross(step, piece).wait_send()
            opposite(piece).wait_send()

    @pl.when(inner)
    def _():
        note.wait_send()

    act(copies, "wait_send")
    act(vcopies, "wait_send")


def body(patches, vorticity, pair_source, pair_offset, pair_count, neighbours):
    hbm = pl.BlockSpec(memory_space=pltpu.HBM)
    vmem = pl.BlockSpec(memory_space=pltpu.VMEM)
    out = jax.ShapeDtypeStruct((1, 2 * COMPONENTS, SLAB, CELL * CELL), F32)
    both = pl.pallas_call(
        functools.partial(kernel, patches),
        out_shape=out,
        in_specs=[hbm] * 5,
        out_specs=vmem,
        scratch_shapes=[
            pltpu.SMEM((1, NEAR), jnp.int32),
            pltpu.SMEM((1, NEAR), jnp.int32),
            pltpu.SMEM((1,), jnp.int32),
            pltpu.SMEM((1, 6), jnp.int32),
            pltpu.VMEM((1, COMPONENTS, SLAB, CELL * CELL), BF16),
            pltpu.VMEM((3, PATCH_ROWS, TILE), BF16),
            pltpu.VMEM((4 * TERMS, TILE, TILE), BF16),
            pltpu.VMEM((4 * TERMS, TILE, TILE), BF16),
            pltpu.VMEM((4, HALO, 128), BF16),
            pltpu.VMEM((TERMS, PATCH_ROWS, TILE), BF16),
            pltpu.VMEM((2, 12, 128, TILE), BF16),
            pltpu.VMEM((3, 12, HALO, TILE), F32),
            pltpu.VMEM((COMPONENTS, 128, 128), F32),
            pltpu.VMEM((COMPONENTS, 128, 128), F32),
            pltpu.VMEM((COMPONENTS, 64, 128), F32),
            pltpu.VMEM((4, 12, 8, 128), F32),
            pltpu.VMEM((1, 12, 8, 128), F32),
            pltpu.VMEM((3, 11, 8, 128), F32),
            pltpu.VMEM((2, 8, TILE), jnp.int32),
            pltpu.SemaphoreType.DMA((5,)),
            pltpu.SemaphoreType.DMA((3, PIECES)),
            pltpu.SemaphoreType.DMA((MEMBERS, PIECES)),
            pltpu.SemaphoreType.DMA((MEMBERS, PIECES)),
            pltpu.SemaphoreType.DMA((3 * MEMBERS, PIECES)),
            pltpu.SemaphoreType.DMA((2,)),
            pltpu.SemaphoreType.DMA((2,)),
            pltpu.SemaphoreType.DMA((2,)),
            pltpu.SemaphoreType.DMA((2,)),
            pltpu.SemaphoreType.DMA((1,)),
            pltpu.SemaphoreType.DMA((1,)),
        ],
        compiler_params=pltpu.CompilerParams(
            collective_id=0, has_side_effects=True, vmem_limit_bytes=40 << 20
        ),
    )(pair_source, pair_offset, pair_count, neighbours, vorticity)
    return both[:, :3], both[:, 3:]


def solution(mesh):
    return jax.shard_map(
        functools.partial(body, mesh.shape["patch"]),
        mesh=mesh,
        in_specs=(
            P("patch", None, "comp", None),
            P("patch", None),
            P("patch", None),
            P("patch"),
            P("patch", None),
        ),
        out_specs=(P("patch", None, "comp", None), P("patch", None, "comp", None)),
        check_vma=False,
    )
```
